128 devices in a mesh: space: 64 (over z, y, x_lo, core), tm: 2 (over x_hi).
Axes of the slice: x: 4 (x_hi: 2, x_lo: 2; x = x_hi * 2 + x_lo), y: 4, z: 4, core: 2. Of those that a mesh axis runs over, the one named last changes fastest.
Arguments:
- hidden: bfloat16 [2, 4, 8192, 4096], P(None, None, ('space', 'tm')), may hold values from -6 to 6
- modulation: float32 [2, 4096], replicated, may hold values from -3 to 3
- w_proj: bfloat16 [4096, 64], replicated, may hold values from -0.09375 to 0.09375
- b_proj: float32 [64], replicated, may hold values from -2 to 2
- guidance: float32 [1], replicated, may hold values from 1.5 to 3
- x_noisy: float32 [4, 256, 128, 16], P('tm', 'space'), may hold values from -6 to 6
- sigma: float32 [1], replicated, may hold values from 0.3 to 0.8
- w_in: bfloat16 [3, 3, 48, 512], replicated, may hold values from -0.3125 to 0.3125
- b_in: float32 [512], replicated, may hold values from -2 to 2
- gain: float32 [512], replicated, may hold values from 0.1 to 1.9
- w_mid: bfloat16 [3, 3, 1536, 512], replicated, may hold values from -0.0546875 to 0.0546875
- b_mid: float32 [512], replicated, may hold values from -2 to 2
- w_up: bfloat16 [3, 1536, 512], replicated, may hold values from -0.09375 to 0.09375
- b_up: float32 [512], replicated, may hold values from -2 to 2
Outputs:
- decoded: bfloat16 [4, 512, 256, 512], P('tm', 'space')
The draws below stay inside these ranges and needn't reach their ends.
All inputs are finite; a program needn't handle non-finite values.
Results may differ from the reference program's by a relative error of at most 0.015.
Values may be sent and summed in bfloat16 or wider, within the bound.
A program may use at most 192 MiB of HBM per device.

```python
import jax
import jax.numpy as jnp
from jax import lax

D = 4096
LAT = 16
CH = 512
FRAMES = 4
W = 128
H = 256
SEQ_F = 8192


def steps_of(own_key, dims, pieces, least, top_value):
    level, own = 1.0, jax.random.fold_in(own_key, 6)
    for dim, shards_of in pieces:
        steps = jnp.exp(jax.random.uniform(jax.random.fold_in(own, dim), (shards_of,), jnp.float32, least / len(pieces), top_value / len(pieces)))
        level = level * jnp.repeat(steps, dims[dim] // shards_of).reshape([-1 if axis == dim else 1 for axis in range(len(dims))])
    return level


def centred(stream_key, shape, scale, limit, shards=(), held_as=jnp.bfloat16):
    level = steps_of(stream_key, shape, shards, -0.22, 0.18) if shards else 1.0
    result = jax.random.normal(stream_key, shape, jnp.float32) * scale * level
    return jnp.minimum(jnp.maximum(result, -limit), limit).astype(held_as)


def setup_inputs(seed: int = 0) -> dict:
    streams_of = jax.random.split(jax.random.key(seed), 15)
    hidden = centred(streams_of[0], (2, FRAMES, SEQ_F, D), 1.0, 6.0, ((2, 128),))
    modulation = centred(streams_of[1], (2, D), 0.5, 3.0, (), jnp.float32)
    w_proj = centred(streams_of[2], (D, 4 * LAT), D ** -0.5, 0.09375)
    b_proj = centred(streams_of[3], (4 * LAT,), 0.3, 2.0, (), jnp.float32)
    guidance = jnp.clip(jax.random.uniform(streams_of[4], (1,), jnp.float32, 1.5, 3.0), 1.5, 3.0)
    x_noisy = centred(streams_of[5], (FRAMES, H, W, LAT), 1.0, 6.0, ((0, 2), (1, 64)), jnp.float32)
    sigma = jnp.clip(jax.random.uniform(streams_of[6], (1,), jnp.float32, 0.3, 0.8), 0.3, 0.8)
    w_in = centred(streams_of[7], (3, 3, 3 * LAT, CH), (27 * LAT) ** -0.5, 0.3125)
    b_in = centred(streams_of[8], (CH,), 0.3, 2.0, (), jnp.float32)
    gain = jnp.clip(1.0 + 0.18 * jax.random.normal(streams_of[9], (CH,), jnp.float32), 0.1, 1.9)
    w_mid = centred(streams_of[10], (3, 3, 3 * CH, CH), (27 * CH) ** -0.5, 0.0546875)
    b_mid = centred(streams_of[11], (CH,), 0.3, 2.0, (), jnp.float32)
    w_up = centred(streams_of[12], (3, 3 * CH, CH), (9 * CH) ** -0.5, 0.09375)
    b_up = centred(streams_of[13], (CH,), 0.3, 2.0, (), jnp.float32)
    return dict(hidden=hidden, modulation=modulation, w_proj=w_proj, b_proj=b_proj, guidance=guidance, x_noisy=x_noisy, sigma=sigma, w_in=w_in, b_in=b_in, gain=gain, w_mid=w_mid, b_mid=b_mid, w_up=w_up, b_up=b_up)


norm_eps = 1e-06

def modulate(hidden, modulation):
    values = hidden.astype(jnp.float32)
    centre = lax.optimization_barrier(jnp.mean(values, axis=-1, keepdims=True))
    spread = lax.optimization_barrier(jnp.mean(jnp.square(values - centre), axis=-1, keepdims=True))
    normed = (values - centre) * lax.rsqrt(spread + norm_eps)
    return (normed * (1.0 + modulation[1]) + modulation[0]).astype(jnp.bfloat16)

def unpatchify(patch_rows, row_count, col_count, lat_count):
    frame_count = patch_rows.shape[0]
    patch_grid = patch_rows.reshape(frame_count, row_count // 2, col_count // 2, 2, 2, lat_count)
    return patch_grid.transpose(0, 1, 3, 2, 4, 5).reshape(frame_count, row_count, col_count, lat_count)

def apply_taps(padded, weight, frame_count, row_count, col_count):
    tap_depth = weight.shape[0]
    channels = padded.shape[-1]
    accumulated = jnp.zeros((frame_count * row_count * col_count, weight.shape[-1]), jnp.float32)
    for step_t in range(tap_depth):
        for step_h in range(3):
            block_slice = padded[step_t:step_t + frame_count, step_h:step_h + row_count]
            window = jnp.concatenate([block_slice[:, :, step_w:step_w + col_count] for step_w in range(3)], axis=-1)
            accumulated = accumulated + jnp.dot(window.reshape(-1, 3 * channels), weight[step_t, step_h], preferred_element_type=jnp.float32)
    return accumulated.reshape(frame_count, row_count, col_count, weight.shape[-1])

def rms_silu(values, gain):
    wide = values.astype(jnp.float32)
    inverse_rms = lax.rsqrt(lax.optimization_barrier(jnp.mean(jnp.square(wide), axis=-1, keepdims=True)) + norm_eps)
    return jax.nn.silu(wide * inverse_rms * gain).astype(jnp.bfloat16)

def causal_conv(values, weight):
    padded = jnp.pad(values, ((2, 0), (1, 1), (1, 1), (0, 0)))
    return apply_taps(padded, weight, values.shape[0], values.shape[1], values.shape[2])

def upsample_nearest(values):
    return jnp.repeat(jnp.repeat(values, 2, axis=1), 2, axis=2)

def reference(hidden, modulation, w_proj, b_proj, guidance, x_noisy, sigma, w_in, b_in, gain, w_mid, b_mid, w_up, b_up):
    modulated = modulate(hidden, modulation)
    branches = jnp.dot(modulated.reshape(-1, modulated.shape[-1]), w_proj, preferred_element_type=jnp.float32)
    branches = branches.reshape(2, FRAMES, SEQ_F, 4 * LAT) + b_proj
    prediction = branches[1] + guidance[0] * (branches[0] - branches[1])
    velocity = unpatchify(prediction, H, W, LAT)
    latent = (x_noisy - sigma[0] * velocity).astype(jnp.bfloat16)
    first_out = (causal_conv(latent, w_in) + b_in).astype(jnp.bfloat16)
    activated = rms_silu(first_out, gain)
    second = (first_out.astype(jnp.float32) + causal_conv(activated, w_mid) + b_mid).astype(jnp.bfloat16)
    fine_grid = upsample_nearest(second)
    padded = jnp.pad(fine_grid, ((0, 0), (1, 1), (1, 1), (0, 0)))

    def one_frame(frame_block):
        return (apply_taps(frame_block[None], w_up[None], 1, 2 * H, 2 * W)[0] + b_up).astype(jnp.bfloat16)
    return lax.map(one_frame, padded)
```

```python
import functools

import jax
import jax.numpy as jnp
from jax import lax
from jax.experimental import pallas as pl
from jax.experimental.pallas import tpu as pltpu
from jax.sharding import PartitionSpec as P

MESH = pl.DeviceIdType.MESH
norm_eps = 1e-06
bf16, f32 = jnp.bfloat16, jnp.float32
CH = 512
Q = 64


def moved_down(x):
    at = lax.broadcasted_iota(jnp.int32, x.shape, 0)
    return jnp.where(at == 0, 0.0, pltpu.roll(x, 1, 0))


def moved_up(x):
    at = lax.broadcasted_iota(jnp.int32, x.shape, 0)
    return jnp.where(at == x.shape[0] - 1, 0.0, pltpu.roll(x, x.shape[0] - 1, 0))


def latent_kernel(
    h_ref, mod_ref, w_ref, b_ref, g_ref, sigma_ref, x_ref, land,
    hbuf, wbuf, mod, wmat, bias_in, scalars, xall, xt, lat, hsem, ssmall, xlocal, xsend, xrecv, ssem, rsem,
):
    s, t = lax.axis_index("space"), lax.axis_index("tm")
    ns = lax.axis_size("space")
    other = 1 - t
    after, before = lax.rem(s + 1, ns), lax.rem(s + ns - 1, ns)

    small = []
    for n, (a, b) in enumerate(
        ((w_ref, wbuf), (mod_ref, mod), (b_ref, bias_in), (g_ref, scalars.at[0]), (sigma_ref, scalars.at[1]))
    ):
        load = pltpu.make_async_copy(a, b, ssmall.at[n])
        load.start()
        small.append(load)
    loads = []
    for f in range(4):
        load = pltpu.make_async_copy(h_ref.at[:, f], hbuf.at[f], hsem.at[f])
        load.start()
        loads.append(load)
    x_load = pltpu.make_async_copy(x_ref, xall.at[t], xlocal)
    x_load.start()

    land[...] = jnp.zeros(land.shape, bf16)
    peers = [(s, other), (after, 0), (after, 1), (before, 0), (before, 1)]
    barrier = pltpu.get_barrier_semaphore()
    for peer in peers:
        pl.semaphore_signal(barrier, inc=1, device_id=peer, device_id_type=MESH)

    for load in small:
        load.wait()
    scale = 1.0 + mod[1:2, :]
    shift = mod[0:1, :]
    wide = wbuf[...].astype(f32)
    ordered = jnp.concatenate(
        [wide[block * 16 : block * 16 + 16] for block in (0, 2, 1, 3)], axis=0
    )
    both = jnp.concatenate([ordered * scale, ordered], axis=0)
    for k in range(8):
        at = slice(k * 512, (k + 1) * 512)
        wmat[at] = jnp.transpose(both[:, at]).astype(bf16)
    shift_hi = shift.astype(bf16)
    shift_lo = (shift - shift_hi.astype(f32)).astype(bf16)
    row = lax.broadcasted_iota(jnp.int32, (16, shift.shape[1]), 0)
    sums = jnp.where(
        row == 0,
        1.0,
        jnp.where(
            row == 1, shift_hi.astype(f32), jnp.where(row == 2, shift_lo.astype(f32), 0.0)
        ),
    ).astype(bf16)
    lane = lax.broadcasted_iota(jnp.int32, (Q, Q), 1)
    source = ((lane // 16) % 2) * 32 + (lane // 32) * 16 + lane % 16
    one_hot = (lax.broadcasted_iota(jnp.int32, (Q, Q), 0) == source).astype(f32)
    bias = jnp.dot(
        jnp.broadcast_to(bias_in[...], (8, Q)), one_hot,
        preferred_element_type=f32, precision=lax.Precision.HIGHEST,
    )[0:1]

    totals = jnp.dot(sums, wmat[...], preferred_element_type=f32)
    column_sum = totals[0:1, :Q]
    constant = totals[1:2, Q:] + totals[2:3, Q:] + bias

    pl.semaphore_wait(barrier, 5)
    x_copy = pltpu.make_async_remote_copy(
        src_ref=x_ref, dst_ref=xall.at[t], send_sem=xsend, recv_sem=xrecv,
        device_id=(s, other), device_id_type=MESH,
    )
    x_copy.start()

    guidance, sigma = scalars[0], scalars[1]
    predictions = []
    for pair in range(2):
        loads[2 * pair].wait()
        loads[2 * pair + 1].wait()
        product = jnp.dot(
            hbuf[2 * pair : 2 * pair + 2].reshape(4 * Q, 4096), wmat[...],
            preferred_element_type=f32,
        )
        for f in range(2):
            rows = hbuf[2 * pair + f].reshape(2 * Q, 4096)
            pivot = rows[:, 0:1].astype(f32)
            first, second = jnp.zeros((2 * Q, 128), f32), jnp.zeros((2 * Q, 128), f32)
            for k in range(32):
                part = rows[:, k * 128 : (k + 1) * 128].astype(f32) - pivot
                first = first + part
                second = second + part * part
            offset = jnp.sum(first, axis=1, keepdims=True) * (1.0 / 4096)
            spread = jnp.sum(second, axis=1, keepdims=True) * (1.0 / 4096) - offset * offset
            inverse = lax.rsqrt(jnp.maximum(spread, 0.0) + norm_eps)
            own = product[2 * f * Q : 2 * (f + 1) * Q, :Q]
            branch = inverse * (own - (pivot + offset) * column_sum)
            cond, uncond = branch[:Q], branch[Q:]
            predictions.append(uncond + guidance * (cond - uncond) + constant)

    x_load.wait()
    x_copy.wait()
    xt[...] = jnp.transpose(
        jnp.concatenate([xall[f // 2, f % 2, 2 * t + a] for f in range(4) for a in range(2)], axis=0)
    )
    even, odd = xt[pl.ds(0, Q, stride=2), :], xt[pl.ds(1, Q, stride=2), :]
    position = lax.broadcasted_iota(jnp.int32, (Q, Q), 0)
    compact = []
    for f in range(4):
        at = slice(32 * f, 32 * f + 32)
        noisy = jnp.concatenate([even[:, at], odd[:, at]], axis=1)
        latent = noisy - sigma * predictions[f]
        from_left = jnp.where(position == 0, 0.0, pltpu.roll(latent, 1, 0))
        from_right = jnp.where(position == Q - 1, 0.0, pltpu.roll(latent, Q - 1, 0))
        beside = jnp.where(lane < 32, from_right, from_left)
        compact.append(jnp.concatenate([latent, beside], axis=1).astype(bf16))
    to = lax.broadcasted_iota(jnp.int32, (128, 128), 1)
    source = ((to // 16 + 3) % 4) * 32 + (to // 64) * 16 + to % 16
    widen = (lax.broadcasted_iota(jnp.int32, (128, 128), 0) == source).astype(f32).astype(bf16)
    lat[...] = jnp.dot(
        jnp.concatenate(compact, axis=0), widen, preferred_element_type=f32
    ).astype(bf16).reshape(4, Q, 128)

    def send(peer, to, slot, k):
        count = 2 + 2 * to
        return pltpu.make_async_remote_copy(
            src_ref=lat.at[pl.ds(0, count)], dst_ref=land.at[slot, pl.ds(6 - count, count)],
            send_sem=ssem.at[k], recv_sem=rsem.at[slot], device_id=peer, device_id_type=MESH,
        )

    sends = [
        send((before, 1), 1, 4 + t, 0), send((after, 1), 1, t, 1),
        send((before, 0), 0, 4 + t, 2), send((after, 0), 0, t, 3),
    ]
    for to in range(2):
        @pl.when(other == to)
        def _():
            send((s, to), to, 3 - to, 4).start()
    for copy in sends:
        copy.start()

    for me in range(2):
        @pl.when(t == me)
        def _():
            count = 2 + 2 * me
            land[2 + me, 6 - count : 6] = lat[0:count]
            for slot in (3 - me, 0, 1, 4, 5):
                send((s, other), me, slot, 4).wait_recv()
            send((s, other), 1 - me, 2 + me, 4).wait_send()
    for copy in sends:
        copy.wait_send()

    @pl.when(s == 0)
    def _():
        land[0:2] = jnp.zeros((2, 6, Q, 128), bf16)

    @pl.when(s == ns - 1)
    def _():
        land[4:6] = jnp.zeros((2, 6, Q, 128), bf16)


def decoder_kernel(
    lat_ref, win_ref, bin_ref, gain_ref, wmid_ref, bmid_ref, wup_ref, bup_ref, out_ref,
    land, win, vectors, wm, wu, wp, windows, comps, skip, staged, mixed, pending, fine,
    wrow, wphase, spread, phases, lsem, wsem, vsem, msem, usem, osem,
):
    s, t = lax.axis_index("space"), lax.axis_index("tm")
    ns = lax.axis_size("space")
    lat_load = pltpu.make_async_copy(lat_ref, land, lsem)
    lat_load.start()
    others = [pltpu.make_async_copy(win_ref, win, wsem)]
    for n, ref in enumerate((bin_ref, gain_ref, bmid_ref, bup_ref)):
        others.append(pltpu.make_async_copy(ref, vectors.at[n], vsem.at[n]))
    mids = [pltpu.make_async_copy(wmid_ref.at[i], wm.at[i], msem.at[i]) for i in range(3)]
    up_load = pltpu.make_async_copy(wup_ref, wu, usem)
    for load in others + mids + [up_load]:
        load.start()

    wp[...] = jnp.zeros(wp.shape, bf16)
    to = lax.broadcasted_iota(jnp.int32, (256, 256), 0)
    at = lax.broadcasted_iota(jnp.int32, (256, 256), 1)
    spread[...] = jnp.where(
        to == 4 * (at % 64) + 2 * ((at // 64) % 2) + at // 128, 1.0, 0.0
    ).astype(bf16)
    for load in others:
        load.wait()
    for i in range(3):
        for j in range(3):
            block = win[i, j]
            for a in range(2):
                for b in range(2):
                    at = i * 256 + ((a + j - 1) % 4) * 64 + b * 16
                    wp[at : at + 48, (2 * a + b) * CH : (2 * a + b + 1) * CH] = block
    lat_load.wait()
    lane = lax.broadcasted_iota(jnp.int32, (Q, 128), 1)
    for p in range(4):
        for f in range(6):
            beside = jnp.where(
                lane < 64, land[p + 2, f].astype(f32), land[p, f].astype(f32)
            ).astype(bf16)
            windows[p, f] = jnp.concatenate([land[p + 1, f], beside], axis=1)

    bias_first, half_gain = vectors[0], 0.5 * vectors[1]
    bias_mid, bias_up = vectors[2], vectors[3]
    frame = lax.broadcasted_iota(jnp.int32, (4 * Q, 1), 0) // Q
    frame_held = jnp.logical_or(frame >= 2, t > 0)

    def patch_row(p, _):
        lhs = jnp.concatenate(
            [windows[p, i : i + 4].reshape(4 * Q, 256) for i in range(3)], axis=1
        )
        for a in range(2):
            line = 2 * p + a
            held = jnp.logical_and(4 * s - 2 + line >= 0, 4 * s - 2 + line < 4 * ns)
            mask = jnp.where(jnp.logical_and(frame_held, held), 1.0, 0.0)
            sides = []
            for b in range(2):
                column = (2 * a + b) * CH
                value = jnp.dot(
                    lhs, wp[:, column : column + CH], preferred_element_type=f32
                ) + bias_first
                for f in range(2):
                    skip[f, b, line] = value[(2 + f) * Q : (3 + f) * Q].astype(bf16)
                power = jnp.mean(value * value, axis=1, keepdims=True)
                half = value * (lax.rsqrt(power + norm_eps) * mask) * half_gain
                active = half * jnp.tanh(half) + half
                a0, a1, a2, a3 = [active[f * Q : (f + 1) * Q] for f in range(4)]
                sides.append((a0 - a2, a1 + a2, a2 - a1, a1 - a3))
            for k in range(4):
                even, odd = sides[0][k], sides[1][k]
                comps[4 * k, line] = (moved_down(odd) - odd).astype(bf16)
                comps[4 * k + 1, line] = (even + odd).astype(bf16)
                comps[4 * k + 2, line] = (odd - even).astype(bf16)
                comps[4 * k + 3, line] = (even - moved_up(even)).astype(bf16)
        return 0

    lax.fori_loop(0, 4, patch_row, 0)

    def finish(f, b, n, middle):
        cols = slice(n * 256, (n + 1) * 256)
        for r in range(6):
            line = 4 * s - 1 + r
            held = jnp.where(jnp.logical_and(line >= 0, line < 4 * ns), 1.0, 0.0)
            value = (
                skip[f, b, r + 1, :, cols].astype(f32)
                + middle[r * Q : (r + 1) * Q]
                + bias_mid[:, cols]
            ) * held
            fine[f, r, 1 + b, :, cols] = value.astype(bf16)
            if b == 0:
                fine[f, r, 3, :, cols] = moved_up(value).astype(bf16)
            else:
                fine[f, r, 0, :, cols] = moved_down(value).astype(bf16)

    def phase_weights(a):
        both = (wu.at[1], wu.at[2]) if a == 0 else (wu.at[0], wu.at[1])
        alone = wu.at[2 * a]
        wrow[...] = both[0][...] + both[1][...]
        for i in range(2):
            held = alone if i == a else wrow
            k0, k1, k2 = [held[k * CH : (k + 1) * CH] for k in range(3)]
            for n, value in enumerate((k0, k1 + k2, k0 + k1, k2)):
                wphase[a, i, n] = value

    for k in range(4):
        if k == 0:
            mids[0].wait()
        if k == 1:
            mids[1].wait()
            mids[2].wait()
            up_load.wait()
        if k > 1:
            phase_weights(k - 2)
        source = wm.at[0] if k == 0 else wm.at[2] if k == 3 else staged
        if k in (1, 2):
            for j in range(3):
                ends = wm[0, j] + wm[2, j]
                staged[j] = ends + wm[1, j] if k == 1 else ends - wm[1, j]
        for j in range(3):
            left, centre, right = [source[j, c * CH : (c + 1) * CH] for c in range(3)]
            mixed[0, j * CH : (j + 1) * CH] = left + right + centre
            mixed[1, j * CH : (j + 1) * CH] = left + right - centre
        for n in range(2):
            cols = slice(n * 256, (n + 1) * 256)
            products = []
            for c in range(4):
                lhs = jnp.concatenate(
                    [comps[4 * k + c, j : j + 6].reshape(6 * Q, CH) for j in range(3)], axis=1
                )
                if c in (1, 2):
                    rhs = mixed[c - 1, :, cols]
                else:
                    at = 0 if c == 0 else 2 * CH
                    rhs = jnp.concatenate(
                        [source[j, at : at + CH, cols] for j in range(3)], axis=0
                    )
                products.append(jnp.dot(lhs, rhs, preferred_element_type=f32))
            m0, m1, m2, m3 = products
            for b, total in enumerate((m0 + 0.5 * (m1 + m2), 0.5 * (m1 - m2) - m3)):
                if k == 0:
                    pending[0, b, :, cols] = total
                elif k == 1:
                    pending[1, b, :, cols] = total
                elif k == 2:
                    held = pending[1, b, :, cols]
                    pending[1, b, :, cols] = 0.5 * (held - total)
                    finish(0, b, n, pending[0, b, :, cols] + 0.5 * (held + total))
                else:
                    finish(1, b, n, pending[1, b, :, cols] - total)

    writes = []

    def order_lines(f, a):
        lines = jnp.dot(
            spread[...],
            jnp.concatenate([phases[f, r].reshape(256, CH) for r in range(4)], axis=1),
            preferred_element_type=f32,
        ).astype(bf16)
        base = 8 * a + 4 * f
        for r in range(4):
            comps[base + r, 0:4] = lines[:, r * CH : (r + 1) * CH].reshape(4, Q, CH)
        write = pltpu.make_async_copy(
            comps.at[base : base + 4, 0:4], out_ref.at[f, :, a], osem.at[2 * a + f]
        )
        write.start()
        writes.append(write)

    behind = None
    for a in range(2):
        for f in range(2):
            for n in range(2):
                cols = slice(n * 256, (n + 1) * 256)
                for b in range(2):
                    lhs = jnp.concatenate(
                        [
                            fine[f, a + i : a + i + 4, b + c : b + c + 2].reshape(8 * Q, CH)
                            for i in range(2)
                            for c in range(2)
                        ],
                        axis=1,
                    )
                    rhs = wphase[a, :, 2 * b : 2 * b + 2, :, cols].reshape(4 * CH, 256)
                    value = jnp.dot(lhs, rhs, preferred_element_type=f32) + bias_up[:, cols]
                    phases[f, :, b, :, cols] = value.astype(bf16).reshape(4, 2 * Q, 256)
            if behind is not None:
                order_lines(*behind)
            behind = (f, a)
    order_lines(*behind)
    for write in writes:
        write.wait()


def on_device(
    hidden, modulation, w_proj, b_proj, guidance, x_noisy, sigma, w_in, b_in, gain,
    w_mid, b_mid, w_up, b_up,
):
    vmem = pl.BlockSpec(memory_space=pltpu.VMEM)
    anywhere = pl.BlockSpec(memory_space=pltpu.HBM)
    rows = lambda v: v.reshape(1, -1)
    dma = pltpu.SemaphoreType.DMA
    latents = pl.pallas_call(
        latent_kernel,
        out_shape=jax.ShapeDtypeStruct((6, 6, Q, 128), bf16),
        in_specs=[anywhere] * 7,
        out_specs=vmem,
        scratch_shapes=[
            pltpu.VMEM((4, 2, Q, 4096), bf16),
            pltpu.VMEM((64, 4096), bf16),
            pltpu.VMEM((2, 4096), f32),
            pltpu.VMEM((4096, 128), bf16),
            pltpu.VMEM((1, 64), f32),
            pltpu.VMEM((2, 1, 1), f32),
            pltpu.VMEM((2, 2, 4, 16, 128), f32),
            pltpu.VMEM((128, 128), f32),
            pltpu.VMEM((4, Q, 128), bf16),
            dma((4,)), dma((5,)), dma, dma, dma, dma((5,)), dma((6,)),
        ],
        compiler_params=pltpu.CompilerParams(
            collective_id=0, has_side_effects=True, vmem_limit_bytes=60 << 20
        ),
    )(
        hidden, modulation, w_proj.T, rows(b_proj), rows(guidance), rows(sigma),
        jnp.swapaxes(x_noisy, 2, 3),
    )
    decoded = pl.pallas_call(
        decoder_kernel,
        out_shape=jax.ShapeDtypeStruct((2, 4, 2, 4, Q, CH), bf16),
        in_specs=[anywhere] * 8,
        out_specs=anywhere,
        scratch_shapes=[
            pltpu.VMEM((6, 6, Q, 128), bf16),
            pltpu.VMEM((3, 3, 48, CH), bf16),
            pltpu.VMEM((4, 1, CH), f32),
            pltpu.VMEM((3, 3, 3 * CH, CH), bf16),
            pltpu.VMEM((3, 3 * CH, CH), bf16),
            pltpu.VMEM((768, 4 * CH), bf16),
            pltpu.VMEM((4, 6, Q, 256), bf16),
            pltpu.VMEM((16, 8, Q, CH), bf16),
            pltpu.VMEM((2, 2, 8, Q, CH), bf16),
            pltpu.VMEM((3, 3 * CH, CH), bf16),
            pltpu.VMEM((2, 3 * CH, CH), bf16),
            pltpu.VMEM((2, 2, 6 * Q, CH), f32),
            pltpu.VMEM((2, 6, 4, Q, CH), bf16),
            pltpu.VMEM((3 * CH, CH), bf16),
            pltpu.VMEM((2, 2, 4, CH, CH), bf16),
            pltpu.VMEM((256, 256), bf16),
            pltpu.VMEM((2, 4, 2, 2 * Q, CH), bf16),
            dma, dma, dma((4,)), dma((3,)), dma, dma((4,)),
        ],
        compiler_params=pltpu.CompilerParams(vmem_limit_bytes=62 << 20),
    )(latents, w_in, rows(b_in), rows(gain), w_mid, rows(b_mid), w_up, rows(b_up))
    return decoded.reshape(2, 8, 256, CH)


def solution(mesh):
    return jax.shard_map(
        on_device,
        mesh=mesh,
        in_specs=(
            P(None, None, ("space", "tm"), None), P(), P(), P(), P(),
            P("tm", "space", None, None), P(), P(), P(), P(), P(), P(), P(), P(),
        ),
        out_specs=P("tm", "space", None, None),
        check_vma=False,
    )
```

```python
import functools

import jax
import jax.numpy as jnp
from jax import lax
from jax.experimental import pallas as pl
from jax.experimental.pallas import tpu as pltpu
from jax.sharding import PartitionSpec as P

MESH = pl.DeviceIdType.MESH
norm_eps = 1e-06
bf16, f32 = jnp.bfloat16, jnp.float32
CH = 512
Q = 64


def moved_down(x):
    at = lax.broadcasted_iota(jnp.int32, x.shape, 0)
    return jnp.where(at == 0, 0.0, pltpu.roll(x, 1, 0))


def moved_up(x):
    at = lax.broadcasted_iota(jnp.int32, x.shape, 0)
    return jnp.where(at == x.shape[0] - 1, 0.0, pltpu.roll(x, x.shape[0] - 1, 0))


def latent_kernel(
    h_ref, mod_ref, w_ref, b_ref, g_ref, sigma_ref, x_ref, windows,
    hbuf, wbuf, mod, wmat, bias_in, scalars, xall, xt, lat, land,
    hsem, ssmall, xlocal, xsend, xrecv, ssem, rsem,
):
    s, t = lax.axis_index("space"), lax.axis_index("tm")
    ns = lax.axis_size("space")
    other = 1 - t
    after, before = s + 1, s - 1

    small = []
    for n, (a, b) in enumerate(
        ((w_ref, wbuf), (mod_ref, mod), (b_ref, bias_in), (g_ref, scalars.at[0]), (sigma_ref, scalars.at[1]))
    ):
        load = pltpu.make_async_copy(a, b, ssmall.at[n])
        load.start()
        small.append(load)
    loads = []
    for f in range(4):
        load = pltpu.make_async_copy(h_ref.at[:, f], hbuf.at[f], hsem.at[f])
        load.start()
        loads.append(load)
    x_load = pltpu.make_async_copy(x_ref, xall.at[t], xlocal)
    x_load.start()

    land[...] = jnp.zeros(land.shape, bf16)
    barrier = pltpu.get_barrier_semaphore()
    pl.semaphore_signal(barrier, inc=1, device_id=(s, other), device_id_type=MESH)
    for held, row in ((s > 0, before), (s < ns - 1, after)):
        @pl.when(held)
        def _():
            for k in range(2):
                pl.semaphore_signal(barrier, inc=1, device_id=(row, k), device_id_type=MESH)

    for load in small:
        load.wait()
    scale = 1.0 + mod[1:2, :]
    shift = mod[0:1, :]
    wide = wbuf[...].astype(f32)
    ordered = jnp.concatenate(
        [wide[block * 16 : block * 16 + 16] for block in (0, 2, 1, 3)], axis=0
    )
    both = jnp.concatenate([ordered * scale, ordered], axis=0)
    for k in range(8):
        at = slice(k * 512, (k + 1) * 512)
        wmat[at] = jnp.transpose(both[:, at]).astype(bf16)
    shift_hi = shift.astype(bf16)
    shift_lo = (shift - shift_hi.astype(f32)).astype(bf16)
    row = lax.broadcasted_iota(jnp.int32, (16, shift.shape[1]), 0)
    sums = jnp.where(
        row == 0,
        1.0,
        jnp.where(
            row == 1, shift_hi.astype(f32), jnp.where(row == 2, shift_lo.astype(f32), 0.0)
        ),
    ).astype(bf16)
    lane = lax.broadcasted_iota(jnp.int32, (Q, Q), 1)
    source = ((lane // 16) % 2) * 32 + (lane // 32) * 16 + lane % 16
    one_hot = (lax.broadcasted_iota(jnp.int32, (Q, Q), 0) == source).astype(f32)
    bias = jnp.dot(
        jnp.broadcast_to(bias_in[...], (8, Q)), one_hot,
        preferred_element_type=f32, precision=lax.Precision.HIGHEST,
    )[0:1]

    totals = jnp.dot(sums, wmat[...], preferred_element_type=f32)
    column_sum = totals[0:1, :Q]
    constant = totals[1:2, Q:] + totals[2:3, Q:] + bias

    pl.semaphore_wait(
        barrier, 1 + 2 * (s > 0).astype(jnp.int32) + 2 * (s < ns - 1).astype(jnp.int32)
    )
    x_copy = pltpu.make_async_remote_copy(
        src_ref=x_ref, dst_ref=xall.at[t], send_sem=xsend, recv_sem=xrecv,
        device_id=(s, other), device_id_type=MESH,
    )
    x_copy.start()

    guidance, sigma = scalars[0], scalars[1]
    predictions = []
    for pair in range(2):
        loads[2 * pair].wait()
        loads[2 * pair + 1].wait()
        product = jnp.dot(
            hbuf[2 * pair : 2 * pair + 2].reshape(4 * Q, 4096), wmat[...],
            preferred_element_type=f32,
        )
        for f in range(2):
            rows = hbuf[2 * pair + f].reshape(2 * Q, 4096)
            pivot = rows[:, 0:1].astype(f32)
            first, second = jnp.zeros((2 * Q, 128), f32), jnp.zeros((2 * Q, 128), f32)
            for k in range(32):
                part = rows[:, k * 128 : (k + 1) * 128].astype(f32) - pivot
                first = first + part
                second = second + part * part
            offset = jnp.sum(first, axis=1, keepdims=True) * (1.0 / 4096)
            spread = jnp.sum(second, axis=1, keepdims=True) * (1.0 / 4096) - offset * offset
            inverse = lax.rsqrt(jnp.maximum(spread, 0.0) + norm_eps)
            own = product[2 * f * Q : 2 * (f + 1) * Q, :Q]
            branch = inverse * (own - (pivot + offset) * column_sum)
            cond, uncond = branch[:Q], branch[Q:]
            predictions.append(uncond + guidance * (cond - uncond) + constant)

    x_load.wait()
    x_copy.wait()
    xt[...] = jnp.transpose(
        jnp.concatenate([xall[f // 2, f % 2, 2 * t + a] for f in range(4) for a in range(2)], axis=0)
    )
    even, odd = xt[pl.ds(0, Q, stride=2), :], xt[pl.ds(1, Q, stride=2), :]
    position = lax.broadcasted_iota(jnp.int32, (Q, Q), 0)
    compact = []
    for f in range(4):
        at = slice(32 * f, 32 * f + 32)
        noisy = jnp.concatenate([even[:, at], odd[:, at]], axis=1)
        latent = noisy - sigma * predictions[f]
        from_left = jnp.where(position == 0, 0.0, pltpu.roll(latent, 1, 0))
        from_right = jnp.where(position == Q - 1, 0.0, pltpu.roll(latent, Q - 1, 0))
        beside = jnp.where(lane < 32, from_right, from_left)
        compact.append(jnp.concatenate([latent, beside], axis=1).astype(bf16))
    to = lax.broadcasted_iota(jnp.int32, (128, 128), 1)
    source = ((to // 16 + 3) % 4) * 32 + (to // 64) * 16 + to % 16
    widen = (lax.broadcasted_iota(jnp.int32, (128, 128), 0) == source).astype(f32).astype(bf16)
    lat[...] = jnp.dot(
        jnp.concatenate(compact, axis=0), widen, preferred_element_type=f32
    ).astype(bf16).reshape(4, Q, 128)

    def send(peer, to, slot, k):
        count = 2 + 2 * to
        return pltpu.make_async_remote_copy(
            src_ref=lat.at[pl.ds(0, count)], dst_ref=land.at[slot, pl.ds(6 - count, count)],
            send_sem=ssem.at[k], recv_sem=rsem.at[slot], device_id=peer, device_id_type=MESH,
        )

    def send_row(row, slot, k):
        return [send((row, 1), 1, slot, k), send((row, 0), 0, slot, k + 1)]

    rows_held = ((s > 0, before, 4 + t, 0), (s < ns - 1, after, t, 2))
    for held, row, slot, k in rows_held:
        @pl.when(held)
        def _():
            for copy in send_row(row, slot, k):
                copy.start()
    for to in range(2):
        @pl.when(other == to)
        def _():
            send((s, to), to, 3 - to, 4).start()

    for me in range(2):
        @pl.when(t == me)
        def _():
            count = 2 + 2 * me
            land[2 + me, 6 - count : 6] = lat[0:count]
            send((s, other), me, 3 - me, 4).wait_recv()
            send((s, other), 1 - me, 2 + me, 4).wait_send()
            for held, slots in ((s > 0, (0, 1)), (s < ns - 1, (4, 5))):
                @pl.when(held)
                def _():
                    for slot in slots:
                        send((s, other), me, slot, 4).wait_recv()
    for held, row, slot, k in rows_held:
        @pl.when(held)
        def _():
            for copy in send_row(row, slot, k):
                copy.wait_send()

    wide_lane = lax.broadcasted_iota(jnp.int32, (Q, 128), 1)
    for p in range(4):
        for f in range(6):
            beside = jnp.where(
                wide_lane < 64, land[p + 2, f].astype(f32), land[p, f].astype(f32)
            ).astype(bf16)
            windows[p, f] = jnp.concatenate([land[p + 1, f], beside], axis=1)


def decoder_kernel(
    windows_ref, win_ref, bin_ref, gain_ref, wmid_ref, bmid_ref, wup_ref, bup_ref, out_ref,
    windows, win, wp, vectors, wm, wu, comps, skip, staged, mixed, pending, fine,
    wrow, wphase, spread, phases, lsem, wsem, vsem, msem, usem, osem,
):
    s, t = lax.axis_index("space"), lax.axis_index("tm")
    ns = lax.axis_size("space")
    others = [
        pltpu.make_async_copy(windows_ref, windows, lsem), pltpu.make_async_copy(win_ref, win, wsem)
    ]
    for n, ref in enumerate((bin_ref, gain_ref, bmid_ref, bup_ref)):
        others.append(pltpu.make_async_copy(ref, vectors.at[n], vsem.at[n]))
    for load in others:
        load.start()

    to = lax.broadcasted_iota(jnp.int32, (256, 256), 0)
    at = lax.broadcasted_iota(jnp.int32, (256, 256), 1)
    spread[...] = jnp.where(
        to == 4 * (at % 64) + 2 * ((at // 64) % 2) + at // 128, 1.0, 0.0
    ).astype(bf16)

    wp[...] = jnp.zeros(wp.shape, bf16)
    for load in others:
        load.wait()
    mids = [pltpu.make_async_copy(wmid_ref.at[i], wm.at[i], msem.at[i]) for i in range(3)]
    up_load = pltpu.make_async_copy(wup_ref, wu, usem)
    for load in mids + [up_load]:
        load.start()
    for i in range(3):
        for j in range(3):
            block = win[i, j]
            for a in range(2):
                for b in range(2):
                    at = i * 256 + ((a + j - 1) % 4) * 64 + b * 16
                    wp[at : at + 48, (2 * a + b) * CH : (2 * a + b + 1) * CH] = block

    bias_first, half_gain = vectors[0], 0.5 * vectors[1]
    bias_mid, bias_up = vectors[2], vectors[3]
    frame = lax.broadcasted_iota(jnp.int32, (4 * Q, 1), 0) // Q
    frame_held = jnp.logical_or(frame >= 2, t > 0)

    def patch_row(p, _):
        lhs = jnp.concatenate(
            [windows[p, i : i + 4].reshape(4 * Q, 256) for i in range(3)], axis=1
        )
        for a in range(2):
            line = 2 * p + a
            held = jnp.logical_and(4 * s - 2 + line >= 0, 4 * s - 2 + line < 4 * ns)
            mask = jnp.where(jnp.logical_and(frame_held, held), 1.0, 0.0)
            sides = []
            for b in range(2):
                column = (2 * a + b) * CH
                value = jnp.dot(
                    lhs, wp[:, column : column + CH], preferred_element_type=f32
                ) + bias_first
                for f in range(2):
                    skip[f, b, line] = value[(2 + f) * Q : (3 + f) * Q].astype(bf16)
                power = jnp.mean(value * value, axis=1, keepdims=True)
                half = value * (lax.rsqrt(power + norm_eps) * mask) * half_gain
                active = half * jnp.tanh(half) + half
                a0, a1, a2, a3 = [active[f * Q : (f + 1) * Q] for f in range(4)]
                sides.append((a0 - a2, a1 + a2, a2 - a1, a1 - a3))
            for k in range(4):
                even, odd = sides[0][k], sides[1][k]
                comps[4 * k, line] = (moved_down(odd) - odd).astype(bf16)
                comps[4 * k + 1, line] = (even + odd).astype(bf16)
                comps[4 * k + 2, line] = (odd - even).astype(bf16)
                comps[4 * k + 3, line] = (even - moved_up(even)).astype(bf16)
        return 0

    lax.fori_loop(0, 4, patch_row, 0)

    def finish(f, b, n, middle):
        cols = slice(n * 256, (n + 1) * 256)
        for r in range(6):
            line = 4 * s - 1 + r
            held = jnp.where(jnp.logical_and(line >= 0, line < 4 * ns), 1.0, 0.0)
            value = (
                skip[f, b, r + 1, :, cols].astype(f32)
                + middle[r * Q : (r + 1) * Q]
                + bias_mid[:, cols]
            ) * held
            rounded = value.astype(bf16)
            fine[f, r, b, :, cols] = rounded
            if b == 1:
                odd, even = rounded.astype(f32), fine[f, r, 0, :, cols].astype(f32)
                fine[f, r, 2, :, cols] = (even - moved_down(odd)).astype(bf16)
                fine[f, r, 3, :, cols] = (odd - even).astype(bf16)
                fine[f, r, 4, :, cols] = (moved_up(even) - odd).astype(bf16)

    def phase_weights(a):
        both = (wu.at[1], wu.at[2]) if a == 0 else (wu.at[0], wu.at[1])
        alone = wu.at[2 * a]
        wrow[...] = both[0][...] + both[1][...]
        for i in range(2):
            held = alone if i == a else wrow
            k0, k1, k2 = [held[k * CH : (k + 1) * CH] for k in range(3)]
            for n, value in enumerate((k0, k0 + k1 + k2, k2)):
                wphase[a, n, i] = value

    for k in range(4):
        if k == 0:
            mids[0].wait()
        if k == 1:
            mids[1].wait()
            mids[2].wait()
            up_load.wait()
        if k > 1:
            phase_weights(k - 2)
        source = wm.at[0] if k == 0 else wm.at[2] if k == 3 else staged
        if k in (1, 2):
            for j in range(3):
                ends = wm[0, j] + wm[2, j]
                staged[j] = ends + wm[1, j] if k == 1 else ends - wm[1, j]
        for j in range(3):
            left, centre, right = [source[j, c * CH : (c + 1) * CH] for c in range(3)]
            mixed[0, j * CH : (j + 1) * CH] = left + right + centre
            mixed[1, j * CH : (j + 1) * CH] = left + right - centre
        for n in range(2):
            cols = slice(n * 256, (n + 1) * 256)
            products = []
            for c in range(4):
                lhs = jnp.concatenate(
                    [comps[4 * k + c, j : j + 6].reshape(6 * Q, CH) for j in range(3)], axis=1
                )
                if c in (1, 2):
                    rhs = mixed[c - 1, :, cols]
                else:
                    at = 0 if c == 0 else 2 * CH
                    rhs = jnp.concatenate(
                        [source[j, at : at + CH, cols] for j in range(3)], axis=0
                    )
                products.append(jnp.dot(lhs, rhs, preferred_element_type=f32))
            m0, m1, m2, m3 = products
            for b, total in enumerate((m0 + 0.5 * (m1 + m2), 0.5 * (m1 - m2) - m3)):
                if k == 0:
                    pending[0, b, :, cols] = total
                elif k == 1:
                    pending[1, b, :, cols] = total
                elif k == 2:
                    held = pending[1, b, :, cols]
                    pending[1, b, :, cols] = 0.5 * (held - total)
                    finish(0, b, n, pending[0, b, :, cols] + 0.5 * (held + total))
                else:
                    finish(1, b, n, pending[1, b, :, cols] - total)

    writes = []

    def order_lines(f, a):
        lines = jnp.dot(
            spread[...],
            jnp.concatenate([phases[f, r].reshape(256, CH) for r in range(4)], axis=1),
            preferred_element_type=f32,
        ).astype(bf16)
        base = 8 * a + 4 * f
        for r in range(4):
            comps[base + r, 0:4] = lines[:, r * CH : (r + 1) * CH].reshape(4, Q, CH)
        write = pltpu.make_async_copy(
            comps.at[base : base + 4, 0:4], out_ref.at[f, :, a], osem.at[2 * a + f]
        )
        write.start()
        writes.append(write)

    behind = None
    for a in range(2):
        for f in range(2):
            for n in range(2):
                cols = slice(n * 256, (n + 1) * 256)
                products = []
                for kind, at in enumerate((2, 0, 3)):
                    lhs = jnp.concatenate(
                        [
                            fine[f, a + i : a + i + 4, at : at + 2].reshape(8 * Q, CH)
                            for i in range(2)
                        ],
                        axis=1,
                    )
                    rhs = wphase[a, kind, :, :, cols].reshape(2 * CH, 256)
                    products.append(jnp.dot(lhs, rhs, preferred_element_type=f32))
                first, centre, last = products
                centre = centre + bias_up[:, cols]
                for b, value in enumerate((centre - first, centre + last)):
                    phases[f, :, b, :, cols] = value.astype(bf16).reshape(4, 2 * Q, 256)
            if behind is not None:
                order_lines(*behind)
            behind = (f, a)
    order_lines(*behind)
    for write in writes:
        write.wait()


def on_device(
    hidden, modulation, w_proj, b_proj, guidance, x_noisy, sigma, w_in, b_in, gain,
    w_mid, b_mid, w_up, b_up,
):
    vmem = pl.BlockSpec(memory_space=pltpu.VMEM)
    anywhere = pl.BlockSpec(memory_space=pltpu.HBM)
    rows = lambda v: v.reshape(1, -1)
    dma = pltpu.SemaphoreType.DMA
    windows = pl.pallas_call(
        latent_kernel,
        out_shape=jax.ShapeDtypeStruct((4, 6, Q, 256), bf16),
        in_specs=[anywhere] * 7,
        out_specs=vmem,
        scratch_shapes=[
            pltpu.VMEM((4, 2, Q, 4096), bf16),
            pltpu.VMEM((64, 4096), bf16),
            pltpu.VMEM((2, 4096), f32),
            pltpu.VMEM((4096, 128), bf16),
            pltpu.VMEM((1, 64), f32),
            pltpu.VMEM((2, 1, 1), f32),
            pltpu.VMEM((2, 2, 4, 16, 128), f32),
            pltpu.VMEM((128, 128), f32),
            pltpu.VMEM((4, Q, 128), bf16),
            pltpu.VMEM((6, 6, Q, 128), bf16),
            dma((4,)), dma((5,)), dma, dma, dma, dma((5,)), dma((6,)),
        ],
        compiler_params=pltpu.CompilerParams(
            collective_id=0, has_side_effects=True, vmem_limit_bytes=60 << 20
        ),
    )(
        hidden, modulation, w_proj.T, rows(b_proj), rows(guidance), rows(sigma),
        jnp.swapaxes(x_noisy, 2, 3),
    )
    decoded = pl.pallas_call(
        decoder_kernel,
        out_shape=jax.ShapeDtypeStruct((2, 4, 2, 4, Q, CH), bf16),
        in_specs=[anywhere] * 8,
        out_specs=anywhere,
        scratch_shapes=[
            pltpu.VMEM((4, 6, Q, 256), bf16),
            pltpu.VMEM((3, 3, 48, CH), bf16),
            pltpu.VMEM((768, 4 * CH), bf16),
            pltpu.VMEM((4, 1, CH), f32),
            pltpu.VMEM((3, 3, 3 * CH, CH), bf16),
            pltpu.VMEM((3, 3 * CH, CH), bf16),
            pltpu.VMEM((16, 8, Q, CH), bf16),
            pltpu.VMEM((2, 2, 8, Q, CH), bf16),
            pltpu.VMEM((3, 3 * CH, CH), bf16),
            pltpu.VMEM((2, 3 * CH, CH), bf16),
            pltpu.VMEM((2, 2, 6 * Q, CH), f32),
            pltpu.VMEM((2, 6, 5, Q, CH), bf16),
            pltpu.VMEM((3 * CH, CH), bf16),
            pltpu.VMEM((2, 3, 2, CH, CH), bf16),
            pltpu.VMEM((256, 256), bf16),
            pltpu.VMEM((2, 4, 2, 2 * Q, CH), bf16),
            dma, dma, dma((4,)), dma((3,)), dma, dma((4,)),
        ],
        compiler_params=pltpu.CompilerParams(vmem_limit_bytes=62 << 20),
    )(windows, w_in, rows(b_in), rows(gain), w_mid, rows(b_mid), w_up, rows(b_up))
    return decoded.reshape(2, 8, 256, CH)


def solution(mesh):
    return jax.shard_map(
        on_device,
        mesh=mesh,
        in_specs=(
            P(None, None, ("space", "tm"), None), P(), P(), P(), P(),
            P("tm", "space", None, None), P(), P(), P(), P(), P(), P(), P(), P(),
        ),
        out_specs=P("tm", "space", None, None),
        check_vma=False,
    )
```

```python
import functools

import jax
import jax.numpy as jnp
from jax import lax
from jax.experimental import pallas as pl
from jax.experimental.pallas import tpu as pltpu
from jax.sharding import PartitionSpec as P

MESH = pl.DeviceIdType.MESH
norm_eps = 1e-06
bf16, f32 = jnp.bfloat16, jnp.float32
CH = 512
Q = 64
NT = (((1,), (1,)), ((), ()))


def moved_down(x):
    at = lax.broadcasted_iota(jnp.int32, x.shape, 0)
    return jnp.where(at == 0, 0.0, pltpu.roll(x, 1, 0))


def moved_up(x):
    at = lax.broadcasted_iota(jnp.int32, x.shape, 0)
    return jnp.where(at == x.shape[0] - 1, 0.0, pltpu.roll(x, x.shape[0] - 1, 0))


def latent_kernel(
    h_ref, mod_ref, w_ref, tail_ref, x_ref, windows,
    hbuf, wbuf, mod, wmat, tail, xall, xt, lat, land, wide,
    hsem, ssmall, xlocal, xsend, xrecv, ssem, rsem,
):
    s, t = lax.axis_index("space"), lax.axis_index("tm")
    ns = lax.axis_size("space")
    other = 1 - t
    after, before = s + 1, s - 1

    small = []
    for n, (a, b) in enumerate(((w_ref, wbuf), (mod_ref, mod), (tail_ref, tail))):
        load = pltpu.make_async_copy(a, b, ssmall.at[n])
        load.start()
        small.append(load)
    loads = []
    for f in range(4):
        for k in range(2):
            load = pltpu.make_async_copy(
                h_ref.at[k, f], hbuf.at[(2 * f + k) * Q : (2 * f + k + 1) * Q], hsem.at[2 * f + k]
            )
            load.start()
            loads.append(load)
    x_load = pltpu.make_async_copy(x_ref.at[:, pl.ds(2 * t, 2)], xall.at[t], xlocal)
    x_load.start()

    land[...] = jnp.zeros(land.shape, bf16)
    barrier = pltpu.get_barrier_semaphore()
    pl.semaphore_signal(barrier, inc=1, device_id=(s, other), device_id_type=MESH)
    for held, row in ((s > 0, before), (s < ns - 1, after)):
        @pl.when(held)
        def _():
            for k in range(2):
                pl.semaphore_signal(barrier, inc=1, device_id=(row, k), device_id_type=MESH)

    for load in small:
        load.wait()
    scale = 1.0 + mod[1:2, :]
    shift = mod[0:1, :]
    for n, block in enumerate((0, 2, 1, 3)):
        part = wbuf[block * 16 : block * 16 + 16]
        wmat[n * 16 : n * 16 + 16] = (part.astype(f32) * scale).astype(bf16)
        wmat[64 + n * 16 : 80 + n * 16] = part
    shift_hi = shift.astype(bf16)
    shift_lo = (shift - shift_hi.astype(f32)).astype(bf16)
    row = lax.broadcasted_iota(jnp.int32, (16, shift.shape[1]), 0)
    hbuf[8 * Q :] = jnp.where(
        row == 0,
        1.0,
        jnp.where(
            row == 1, shift_hi.astype(f32), jnp.where(row == 2, shift_lo.astype(f32), 0.0)
        ),
    ).astype(bf16)
    lane = lax.broadcasted_iota(jnp.int32, (Q, Q), 1)
    source = ((lane // 16) % 2) * 32 + (lane // 32) * 16 + lane % 16
    one_hot = (lax.broadcasted_iota(jnp.int32, (Q, Q), 0) == source).astype(f32)
    bias = jnp.dot(
        jnp.broadcast_to(tail[:, :Q], (8, Q)), one_hot,
        preferred_element_type=f32, precision=lax.Precision.HIGHEST,
    )[0:1]
    guidance, sigma = tail[:, Q : Q + 1], tail[:, Q + 1 : Q + 2]

    pl.semaphore_wait(
        barrier, 1 + 2 * (s > 0).astype(jnp.int32) + 2 * (s < ns - 1).astype(jnp.int32)
    )
    x_copy = pltpu.make_async_remote_copy(
        src_ref=x_ref.at[:, pl.ds(2 * other, 2)], dst_ref=xall.at[t], send_sem=xsend,
        recv_sem=xrecv, device_id=(s, other), device_id_type=MESH,
    )
    x_copy.start()

    for load in loads:
        load.wait()
    product = lax.dot_general(hbuf[...], wmat[...], NT, preferred_element_type=f32)
    statistics = []
    for f in range(4):
        rows = hbuf[2 * f * Q : 2 * (f + 1) * Q]
        pivot = rows[:, 0:1].astype(f32)
        first, second = jnp.zeros((2 * Q, 128), f32), jnp.zeros((2 * Q, 128), f32)
        for k in range(32):
            part = rows[:, k * 128 : (k + 1) * 128].astype(f32) - pivot
            first = first + part
            second = second + part * part
        offset = jnp.sum(first, axis=1, keepdims=True) * (1.0 / 4096)
        spread = jnp.sum(second, axis=1, keepdims=True) * (1.0 / 4096) - offset * offset
        statistics.append((pivot + offset, lax.rsqrt(jnp.maximum(spread, 0.0) + norm_eps)))
    column_sum = product[8 * Q : 8 * Q + 1, :Q]
    constant = product[8 * Q + 1 : 8 * Q + 2, Q:] + product[8 * Q + 2 : 8 * Q + 3, Q:] + bias
    predictions = []
    for f in range(4):
        centre, inverse = statistics[f]
        branch = inverse * (product[2 * f * Q : 2 * (f + 1) * Q, :Q] - centre * column_sum)
        cond, uncond = branch[:Q], branch[Q:]
        predictions.append(uncond + guidance * (cond - uncond) + constant)

    x_load.wait()
    x_copy.wait()
    xt[...] = jnp.transpose(xall[...].reshape(128, 128))
    even, odd = xt[pl.ds(0, Q, stride=2), :], xt[pl.ds(1, Q, stride=2), :]
    for pair in range(2):
        latents = []
        for f in (2 * pair, 2 * pair + 1):
            at = slice(32 * f, 32 * f + 32)
            noisy = jnp.concatenate([even[:, at], odd[:, at]], axis=1)
            latents.append(noisy - sigma * predictions[f])
        lat[pair] = jnp.concatenate(latents, axis=1).astype(bf16)

    def send(peer, to, slot, k):
        count = 1 + to
        return pltpu.make_async_remote_copy(
            src_ref=lat.at[pl.ds(0, count)], dst_ref=land.at[slot, pl.ds(3 - count, count)],
            send_sem=ssem.at[k], recv_sem=rsem.at[slot], device_id=peer, device_id_type=MESH,
        )

    def send_row(row, slot, k):
        return [send((row, 1), 1, slot, k), send((row, 0), 0, slot, k + 1)]

    rows_held = ((s > 0, before, 4 + t, 0), (s < ns - 1, after, t, 2))
    for held, row, slot, k in rows_held:
        @pl.when(held)
        def _():
            for copy in send_row(row, slot, k):
                copy.start()
    for to in range(2):
        @pl.when(other == to)
        def _():
            send((s, to), to, 3 - to, 4).start()

    at = lax.broadcasted_iota(jnp.int32, (256, 256), 0)
    to = lax.broadcasted_iota(jnp.int32, (256, 256), 1)
    turn = (to // 16 + 3) % 4
    source = (turn // 2) * 128 + (to // 128) * 64 + (turn % 2) * 32 + ((to // 64) % 2) * 16 + to % 16
    widen = (at == source).astype(f32).astype(bf16)

    for me in range(2):
        @pl.when(t == me)
        def _():
            count = 1 + me
            land[2 + me, 3 - count : 3] = lat[0:count]
            send((s, other), me, 3 - me, 4).wait_recv()
            send((s, other), 1 - me, 2 + me, 4).wait_send()
            for held, slots in ((s > 0, (0, 1)), (s < ns - 1, (4, 5))):
                @pl.when(held)
                def _():
                    for slot in slots:
                        send((s, other), me, slot, 4).wait_recv()
    for held, row, slot, k in rows_held:
        @pl.when(held)
        def _():
            for copy in send_row(row, slot, k):
                copy.wait_send()

    position = lax.broadcasted_iota(jnp.int32, (Q, 128), 0)
    wide_lane = lax.broadcasted_iota(jnp.int32, (Q, 128), 1)
    parts = []
    for p in range(6):
        for pair in range(3):
            here = land[p, pair].astype(f32)
            from_left = jnp.where(position == 0, 0.0, pltpu.roll(here, 1, 0))
            from_right = jnp.where(position == Q - 1, 0.0, pltpu.roll(here, Q - 1, 0))
            beside = jnp.where((wide_lane // 32) % 2 == 0, from_right, from_left)
            parts.append(jnp.concatenate([here, beside], axis=1).astype(bf16))
    wide[...] = jnp.dot(
        jnp.concatenate(parts, axis=0), widen, preferred_element_type=f32
    ).astype(bf16).reshape(6, 3, Q, 256)
    for p in range(4):
        for f in range(6):
            at = slice(f % 2 * 128, f % 2 * 128 + 128)
            beside = jnp.where(
                wide_lane < 64, wide[p + 2, f // 2, :, at].astype(f32), wide[p, f // 2, :, at].astype(f32)
            ).astype(bf16)
            windows[p, f] = jnp.concatenate([wide[p + 1, f // 2, :, at], beside], axis=1)


def decoder_kernel(
    windows_ref, win_ref, bin_ref, gain_ref, wmid_ref, bmid_ref, wup_ref, bup_ref, out_ref,
    windows, win, wp, vectors, wm, wu, comps, skip, staged, mixed, pending, fine,
    wrow, wphase, spread, phases, lsem, wsem, vsem, msem, usem, osem,
):
    s, t = lax.axis_index("space"), lax.axis_index("tm")
    ns = lax.axis_size("space")
    others = [
        pltpu.make_async_copy(windows_ref, windows, lsem), pltpu.make_async_copy(win_ref, win, wsem)
    ]
    for n, ref in enumerate((bin_ref, gain_ref, bmid_ref, bup_ref)):
        others.append(pltpu.make_async_copy(ref, vectors.at[n], vsem.at[n]))
    for load in others:
        load.start()

    to = lax.broadcasted_iota(jnp.int32, (256, 256), 0)
    at = lax.broadcasted_iota(jnp.int32, (256, 256), 1)
    spread[...] = jnp.where(
        to == 4 * (at % 64) + 2 * ((at // 64) % 2) + at // 128, 1.0, 0.0
    ).astype(bf16)

    wp[...] = jnp.zeros(wp.shape, bf16)
    for load in others:
        load.wait()
    mids = [pltpu.make_async_copy(wmid_ref.at[i], wm.at[i], msem.at[i]) for i in range(3)]
    up_load = pltpu.make_async_copy(wup_ref, wu, usem)
    for load in mids + [up_load]:
        load.start()
    for i in range(3):
        for j in range(3):
            block = win[i, j]
            for a in range(2):
                for b in range(2):
                    at = i * 256 + ((a + j - 1) % 4) * 64 + b * 16
                    wp[at : at + 48, (2 * a + b) * CH : (2 * a + b + 1) * CH] = block

    bias_first, half_gain = vectors[0], 0.5 * vectors[1]
    bias_mid, bias_up = vectors[2], vectors[3]
    frame = lax.broadcasted_iota(jnp.int32, (4 * Q, 1), 0) // Q
    frame_held = jnp.logical_or(frame >= 2, t > 0)

    def patch_row(p, _):
        lhs = jnp.concatenate(
            [windows[p, i : i + 4].reshape(4 * Q, 256) for i in range(3)], axis=1
        )
        for a in range(2):
            line = 2 * p + a
            held = jnp.logical_and(4 * s - 2 + line >= 0, 4 * s - 2 + line < 4 * ns)
            mask = jnp.where(jnp.logical_and(frame_held, held), 1.0, 0.0)
            sides = []
            for b in range(2):
                column = (2 * a + b) * CH
                value = jnp.dot(
                    lhs, wp[:, column : column + CH], preferred_element_type=f32
                ) + bias_first
                for f in range(2):
                    skip[f, b, line] = value[(2 + f) * Q : (3 + f) * Q].astype(bf16)
                power = jnp.mean(value * value, axis=1, keepdims=True)
                half = value * (lax.rsqrt(power + norm_eps) * mask) * half_gain
                active = half * jnp.tanh(half) + half
                a0, a1, a2, a3 = [active[f * Q : (f + 1) * Q] for f in range(4)]
                sides.append((a0 - a2, a1 + a2, a2 - a1, a1 - a3))
            for k in range(4):
                even, odd = sides[0][k], sides[1][k]
                comps[4 * k, line] = (moved_down(odd) - odd).astype(bf16)
                comps[4 * k + 1, line] = (even + odd).astype(bf16)
                comps[4 * k + 2, line] = (odd - even).astype(bf16)
                comps[4 * k + 3, line] = (even - moved_up(even)).astype(bf16)
        return 0

    for p in range(4):
        patch_row(p, 0)

    def finish(f, b, n, middle):
        cols = slice(n * 256, (n + 1) * 256)
        for r in range(6):
            line = 4 * s - 1 + r
            held = jnp.where(jnp.logical_and(line >= 0, line < 4 * ns), 1.0, 0.0)
            value = (
                skip[f, b, r + 1, :, cols].astype(f32)
                + middle[r * Q : (r + 1) * Q]
                + bias_mid[:, cols]
            ) * held
            rounded = value.astype(bf16)
            fine[f, r, b, :, cols] = rounded
            if b == 1:
                odd, even = rounded.astype(f32), fine[f, r, 0, :, cols].astype(f32)
                fine[f, r, 2, :, cols] = (even - moved_down(odd)).astype(bf16)
                fine[f, r, 3, :, cols] = (odd - even).astype(bf16)
                fine[f, r, 4, :, cols] = (moved_up(even) - odd).astype(bf16)

    def phase_weights(a):
        both = (wu.at[1], wu.at[2]) if a == 0 else (wu.at[0], wu.at[1])
        alone = wu.at[2 * a]
        wrow[...] = both[0][...] + both[1][...]
        for i in range(2):
            held = alone if i == a else wrow
            k0, k1, k2 = [held[k * CH : (k + 1) * CH] for k in range(3)]
            for n, value in enumerate((k0, k0 + k1 + k2, k2)):
                wphase[a, n, i] = value

    for k in range(4):
        if k == 0:
            mids[0].wait()
        if k == 1:
            mids[1].wait()
            mids[2].wait()
            up_load.wait()
        if k > 1:
            phase_weights(k - 2)
        source = wm.at[0] if k == 0 else wm.at[2] if k == 3 else staged
        if k in (1, 2):
            for j in range(3):
                ends = wm[0, j] + wm[2, j]
                staged[j] = ends + wm[1, j] if k == 1 else ends - wm[1, j]
        for j in range(3):
            left, centre, right = [source[j, c * CH : (c + 1) * CH] for c in range(3)]
            mixed[0, j * CH : (j + 1) * CH] = left + right + centre
            mixed[1, j * CH : (j + 1) * CH] = left + right - centre
        for n in range(2):
            cols = slice(n * 256, (n + 1) * 256)
            products = []
            for c in range(4):
                lhs = jnp.concatenate(
                    [comps[4 * k + c, j : j + 6].reshape(6 * Q, CH) for j in range(3)], axis=1
                )
                if c in (1, 2):
                    rhs = mixed[c - 1, :, cols]
                else:
                    at = 0 if c == 0 else 2 * CH
                    rhs = jnp.concatenate(
                        [source[j, at : at + CH, cols] for j in range(3)], axis=0
                    )
                products.append(jnp.dot(lhs, rhs, preferred_element_type=f32))
            m0, m1, m2, m3 = products
            for b, total in enumerate((m0 + 0.5 * (m1 + m2), 0.5 * (m1 - m2) - m3)):
                if k == 0:
                    pending[0, b, :, cols] = total
                elif k == 1:
                    pending[1, b, :, cols] = total
                elif k == 2:
                    held = pending[1, b, :, cols]
                    pending[1, b, :, cols] = 0.5 * (held - total)
                    finish(0, b, n, pending[0, b, :, cols] + 0.5 * (held + total))
                else:
                    finish(1, b, n, pending[1, b, :, cols] - total)

    writes = []

    def order_lines(f, a):
        lines = jnp.dot(
            spread[...],
            jnp.concatenate([phases[f, r].reshape(256, CH) for r in range(4)], axis=1),
            preferred_element_type=f32,
        ).astype(bf16)
        base = 8 * a + 4 * f
        for r in range(4):
            comps[base + r, 0:4] = lines[:, r * CH : (r + 1) * CH].reshape(4, Q, CH)
        write = pltpu.make_async_copy(
            comps.at[base : base + 4, 0:4], out_ref.at[f, :, a], osem.at[2 * a + f]
        )
        write.start()
        writes.append(write)

    behind = None
    for a in range(2):
        for f in range(2):
            for n in range(2):
                cols = slice(n * 256, (n + 1) * 256)
                products = []
                for kind, at in enumerate((2, 0, 3)):
                    lhs = jnp.concatenate(
                        [
                            fine[f, a + i : a + i + 4, at : at + 2].reshape(8 * Q, CH)
                            for i in range(2)
                        ],
                        axis=1,
                    )
                    rhs = wphase[a, kind, :, :, cols].reshape(2 * CH, 256)
                    products.append(jnp.dot(lhs, rhs, preferred_element_type=f32))
                first, centre, last = products
                centre = centre + bias_up[:, cols]
                for b, value in enumerate((centre - first, centre + last)):
                    phases[f, :, b, :, cols] = value.astype(bf16).reshape(4, 2 * Q, 256)
            if behind is not None:
                order_lines(*behind)
            behind = (f, a)
    order_lines(*behind)
    for write in writes:
        write.wait()


def on_device(
    hidden, modulation, w_proj, b_proj, guidance, x_noisy, sigma, w_in, b_in, gain,
    w_mid, b_mid, w_up, b_up,
):
    vmem = pl.BlockSpec(memory_space=pltpu.VMEM)
    anywhere = pl.BlockSpec(memory_space=pltpu.HBM)
    rows = lambda v: v.reshape(1, -1)
    dma = pltpu.SemaphoreType.DMA
    windows = pl.pallas_call(
        latent_kernel,
        out_shape=jax.ShapeDtypeStruct((4, 6, Q, 256), bf16),
        in_specs=[anywhere] * 5,
        out_specs=vmem,
        scratch_shapes=[
            pltpu.VMEM((8 * Q + 16, 4096), bf16),
            pltpu.VMEM((64, 4096), bf16),
            pltpu.VMEM((2, 4096), f32),
            pltpu.VMEM((128, 4096), bf16),
            pltpu.VMEM((1, 66), f32),
            pltpu.VMEM((2, 2, 2, 16, 128), f32),
            pltpu.VMEM((128, 128), f32),
            pltpu.VMEM((2, Q, 128), bf16),
            pltpu.VMEM((6, 3, Q, 128), bf16),
            pltpu.VMEM((6, 3, Q, 256), bf16),
            dma((8,)), dma((3,)), dma, dma, dma, dma((5,)), dma((6,)),
        ],
        compiler_params=pltpu.CompilerParams(
            collective_id=0, has_side_effects=True, vmem_limit_bytes=60 << 20
        ),
    )(
        hidden, modulation, w_proj.T, rows(jnp.concatenate([b_proj, guidance, sigma])),
        jnp.swapaxes(x_noisy, 2, 3),
    )
    decoded = pl.pallas_call(
        decoder_kernel,
        out_shape=jax.ShapeDtypeStruct((2, 4, 2, 4, Q, CH), bf16),
        in_specs=[anywhere] * 8,
        out_specs=anywhere,
        scratch_shapes=[
            pltpu.VMEM((4, 6, Q, 256), bf16),
            pltpu.VMEM((3, 3, 48, CH), bf16),
            pltpu.VMEM((768, 4 * CH), bf16),
            pltpu.VMEM((4, 1, CH), f32),
            pltpu.VMEM((3, 3, 3 * CH, CH), bf16),
            pltpu.VMEM((3, 3 * CH, CH), bf16),
            pltpu.VMEM((16, 8, Q, CH), bf16),
            pltpu.VMEM((2, 2, 8, Q, CH), bf16),
            pltpu.VMEM((3, 3 * CH, CH), bf16),
            pltpu.VMEM((2, 3 * CH, CH), bf16),
            pltpu.VMEM((2, 2, 6 * Q, CH), f32),
            pltpu.VMEM((2, 6, 5, Q, CH), bf16),
            pltpu.VMEM((3 * CH, CH), bf16),
            pltpu.VMEM((2, 3, 2, CH, CH), bf16),
            pltpu.VMEM((256, 256), bf16),
            pltpu.VMEM((2, 4, 2, 2 * Q, CH), bf16),
            dma, dma, dma((4,)), dma((3,)), dma, dma((4,)),
        ],
        compiler_params=pltpu.CompilerParams(vmem_limit_bytes=62 << 20),
    )(windows, w_in, rows(b_in), rows(gain), w_mid, rows(b_mid), w_up, rows(b_up))
    return decoded.reshape(2, 8, 256, CH)


def solution(mesh):
    return jax.shard_map(
        on_device,
        mesh=mesh,
        in_specs=(
            P(None, None, ("space", "tm"), None), P(), P(), P(), P(),
            P("tm", "space", None, None), P(), P(), P(), P(), P(), P(), P(), P(),
        ),
        out_specs=P("tm", "space", None, None),
        check_vma=False,
    )
```

```python
import functools

import jax
import jax.numpy as jnp
from jax import lax
from jax.experimental import pallas as pl
from jax.experimental.pallas import tpu as pltpu
from jax.sharding import PartitionSpec as P

MESH = pl.DeviceIdType.MESH
norm_eps = 1e-06
bf16, f32 = jnp.bfloat16, jnp.float32
CH = 512
Q = 64
NT = (((1,), (1,)), ((), ()))


def moved_down(x):
    at = lax.broadcasted_iota(jnp.int32, x.shape, 0)
    return jnp.where(at == 0, 0.0, pltpu.roll(x, 1, 0))


def moved_up(x):
    at = lax.broadcasted_iota(jnp.int32, x.shape, 0)
    return jnp.where(at == x.shape[0] - 1, 0.0, pltpu.roll(x, x.shape[0] - 1, 0))


def latent_kernel(
    h_ref, mod_ref, w_ref, b_ref, g_ref, sigma_ref, x_ref, windows,
    hbuf, wbuf, mod, wmat, bias_in, scalars, xall, xt, lat, land, wide,
    hsem, ssmall, xlocal, xsend, xrecv, ssem, rsem,
):
    s, t = lax.axis_index("space"), lax.axis_index("tm")
    ns = lax.axis_size("space")
    other = 1 - t
    after, before = s + 1, s - 1

    small = []
    for n, (a, b) in enumerate(
        ((w_ref, wbuf), (mod_ref, mod), (b_ref, bias_in), (g_ref, scalars.at[0]), (sigma_ref, scalars.at[1]))
    ):
        load = pltpu.make_async_copy(a, b, ssmall.at[n])
        load.start()
        small.append(load)
    loads = []
    for f in range(4):
        for k in range(2):
            load = pltpu.make_async_copy(
                h_ref.at[k, f], hbuf.at[(2 * f + k) * Q : (2 * f + k + 1) * Q], hsem.at[2 * f + k]
            )
            load.start()
            loads.append(load)
    x_load = pltpu.make_async_copy(x_ref.at[:, pl.ds(2 * t, 2)], xall.at[t], xlocal)
    x_load.start()

    land[...] = jnp.zeros(land.shape, bf16)
    barrier = pltpu.get_barrier_semaphore()
    pl.semaphore_signal(barrier, inc=1, device_id=(s, other), device_id_type=MESH)
    for held, row in ((s > 0, before), (s < ns - 1, after)):
        @pl.when(held)
        def _():
            for k in range(2):
                pl.semaphore_signal(barrier, inc=1, device_id=(row, k), device_id_type=MESH)

    pl.semaphore_wait(
        barrier, 1 + 2 * (s > 0).astype(jnp.int32) + 2 * (s < ns - 1).astype(jnp.int32)
    )
    x_copy = pltpu.make_async_remote_copy(
        src_ref=x_ref.at[:, pl.ds(2 * other, 2)], dst_ref=xall.at[t], send_sem=xsend,
        recv_sem=xrecv, device_id=(s, other), device_id_type=MESH,
    )
    x_copy.start()

    for load in small:
        load.wait()
    scale = 1.0 + mod[1:2, :]
    shift = mod[0:1, :]
    for n, block in enumerate((0, 2, 1, 3)):
        part = wbuf[block * 16 : block * 16 + 16]
        wmat[n * 16 : n * 16 + 16] = (part.astype(f32) * scale).astype(bf16)
        wmat[64 + n * 16 : 80 + n * 16] = part
    shift_hi = shift.astype(bf16)
    shift_lo = (shift - shift_hi.astype(f32)).astype(bf16)
    row = lax.broadcasted_iota(jnp.int32, (16, shift.shape[1]), 0)
    hbuf[8 * Q :] = jnp.where(
        row == 0,
        1.0,
        jnp.where(
            row == 1, shift_hi.astype(f32), jnp.where(row == 2, shift_lo.astype(f32), 0.0)
        ),
    ).astype(bf16)
    lane = lax.broadcasted_iota(jnp.int32, (Q, Q), 1)
    source = ((lane // 16) % 2) * 32 + (lane // 32) * 16 + lane % 16
    one_hot = (lax.broadcasted_iota(jnp.int32, (Q, Q), 0) == source).astype(f32)
    bias = jnp.dot(
        jnp.broadcast_to(bias_in[...], (8, Q)), one_hot,
        preferred_element_type=f32, precision=lax.Precision.HIGHEST,
    )[0:1]
    guidance, sigma = scalars[0], scalars[1]

    for load in loads:
        load.wait()
    product = lax.dot_general(hbuf[...], wmat[...], NT, preferred_element_type=f32)
    statistics = []
    for f in range(4):
        rows = hbuf[2 * f * Q : 2 * (f + 1) * Q]
        pivot = rows[:, 0:1].astype(f32)
        first, second = jnp.zeros((2 * Q, 128), f32), jnp.zeros((2 * Q, 128), f32)
        for k in range(32):
            part = rows[:, k * 128 : (k + 1) * 128].astype(f32) - pivot
            first = first + part
            second = second + part * part
        offset = jnp.sum(first, axis=1, keepdims=True) * (1.0 / 4096)
        spread = jnp.sum(second, axis=1, keepdims=True) * (1.0 / 4096) - offset * offset
        statistics.append((pivot + offset, lax.rsqrt(jnp.maximum(spread, 0.0) + norm_eps)))
    column_sum = product[8 * Q : 8 * Q + 1, :Q]
    constant = product[8 * Q + 1 : 8 * Q + 2, Q:] + product[8 * Q + 2 : 8 * Q + 3, Q:] + bias
    predictions = []
    for f in range(4):
        centre, inverse = statistics[f]
        branch = inverse * (product[2 * f * Q : 2 * (f + 1) * Q, :Q] - centre * column_sum)
        cond, uncond = branch[:Q], branch[Q:]
        predictions.append(uncond + guidance * (cond - uncond) + constant)

    x_load.wait()
    x_copy.wait()
    xt[...] = jnp.transpose(xall[...].reshape(128, 128))
    even, odd = xt[pl.ds(0, Q, stride=2), :], xt[pl.ds(1, Q, stride=2), :]
    for pair in range(2):
        latents = []
        for f in (2 * pair, 2 * pair + 1):
            at = slice(32 * f, 32 * f + 32)
            noisy = jnp.concatenate([even[:, at], odd[:, at]], axis=1)
            latents.append(noisy - sigma * predictions[f])
        lat[pair] = jnp.concatenate(latents, axis=1).astype(bf16)

    def send(peer, to, slot, k):
        count = 1 + to
        return pltpu.make_async_remote_copy(
            src_ref=lat.at[pl.ds(0, count)], dst_ref=land.at[slot, pl.ds(3 - count, count)],
            send_sem=ssem.at[k], recv_sem=rsem.at[slot], device_id=peer, device_id_type=MESH,
        )

    def send_row(row, slot, k):
        return [send((row, 1), 1, slot, k), send((row, 0), 0, slot, k + 1)]

    rows_held = ((s > 0, before, 4 + t, 0), (s < ns - 1, after, t, 2))
    for held, row, slot, k in rows_held:
        @pl.when(held)
        def _():
            for copy in send_row(row, slot, k):
                copy.start()
    for to in range(2):
        @pl.when(other == to)
        def _():
            send((s, to), to, 3 - to, 4).start()

    at = lax.broadcasted_iota(jnp.int32, (256, 256), 0)
    to = lax.broadcasted_iota(jnp.int32, (256, 256), 1)
    turn = (to // 16 + 3) % 4
    source = (turn // 2) * 128 + (to // 128) * 64 + (turn % 2) * 32 + ((to // 64) % 2) * 16 + to % 16
    widen = (at == source).astype(f32).astype(bf16)

    for me in range(2):
        @pl.when(t == me)
        def _():
            count = 1 + me
            land[2 + me, 3 - count : 3] = lat[0:count]
            send((s, other), me, 3 - me, 4).wait_recv()
            send((s, other), 1 - me, 2 + me, 4).wait_send()
            for held, slots in ((s > 0, (0, 1)), (s < ns - 1, (4, 5))):
                @pl.when(held)
                def _():
                    for slot in slots:
                        send((s, other), me, slot, 4).wait_recv()
    for held, row, slot, k in rows_held:
        @pl.when(held)
        def _():
            for copy in send_row(row, slot, k):
                copy.wait_send()

    position = lax.broadcasted_iota(jnp.int32, (Q, 128), 0)
    wide_lane = lax.broadcasted_iota(jnp.int32, (Q, 128), 1)
    parts = []
    for p in range(6):
        for pair in (1, 2):
            here = land[p, pair].astype(f32)
            from_left = jnp.where(position == 0, 0.0, pltpu.roll(here, 1, 0))
            from_right = jnp.where(position == Q - 1, 0.0, pltpu.roll(here, Q - 1, 0))
            beside = jnp.where((wide_lane // 32) % 2 == 0, from_right, from_left)
            parts.append(jnp.concatenate([here, beside], axis=1).astype(bf16))
    wide[...] = jnp.dot(
        jnp.concatenate(parts, axis=0), widen, preferred_element_type=f32
    ).astype(bf16).reshape(6, 2, Q, 256)
    for p in range(4):
        windows[p, 0:2] = jnp.zeros((2, Q, 256), bf16)
        for f in range(2, 6):
            at = slice(f % 2 * 128, f % 2 * 128 + 128)
            above, own, below = [wide[p + k, f // 2 - 1, :, at] for k in range(3)]
            beside = jnp.where(wide_lane < 64, below.astype(f32), above.astype(f32)).astype(bf16)
            windows[p, f] = jnp.concatenate([own, beside], axis=1)


def decoder_kernel(
    windows_ref, win_ref, bin_ref, gain_ref, wmid_ref, bmid_ref, wup_ref, bup_ref, out_ref,
    windows, win, wp, vectors, wm, wu, comps, skip, staged, mixed, pending, fine,
    wrow, wphase, stage, lsem, wsem, vsem, msem, usem, osem,
):
    s, t = lax.axis_index("space"), lax.axis_index("tm")
    ns = lax.axis_size("space")
    others = [
        pltpu.make_async_copy(windows_ref, windows, lsem), pltpu.make_async_copy(win_ref, win, wsem)
    ]
    for n, ref in enumerate((bin_ref, gain_ref, bmid_ref, bup_ref)):
        others.append(pltpu.make_async_copy(ref, vectors.at[n], vsem.at[n]))
    for load in others:
        load.start()

    wp[...] = jnp.zeros(wp.shape, bf16)
    for load in others:
        load.wait()
    mids = [pltpu.make_async_copy(wmid_ref.at[i], wm.at[i], msem.at[i]) for i in range(3)]
    up_load = pltpu.make_async_copy(wup_ref, wu, usem)
    for load in mids + [up_load]:
        load.start()
    for i in range(3):
        for j in range(3):
            block = win[i, j]
            for a in range(2):
                for b in range(2):
                    at = i * 256 + ((a + j - 1) % 4) * 64 + b * 16
                    wp[at : at + 48, (2 * a + b) * CH : (2 * a + b + 1) * CH] = block

    bias_first, half_gain = vectors[0], 0.5 * vectors[1]
    bias_mid, bias_up = vectors[2], vectors[3]
    frame = lax.broadcasted_iota(jnp.int32, (4 * Q, 1), 0) // Q
    frame_held = jnp.logical_or(frame >= 2, t > 0)

    def patch_row(p, _):
        lhs = jnp.concatenate(
            [windows[p, i : i + 4].reshape(4 * Q, 256) for i in range(3)], axis=1
        )
        for a in range(2):
            line = 2 * p + a
            held = jnp.logical_and(4 * s - 2 + line >= 0, 4 * s - 2 + line < 4 * ns)
            mask = jnp.where(jnp.logical_and(frame_held, held), 1.0, 0.0)
            sides = []
            for b in range(2):
                column = (2 * a + b) * CH
                value = jnp.dot(
                    lhs, wp[:, column : column + CH], preferred_element_type=f32
                ) + bias_first
                for f in range(2):
                    skip[f, b, line] = value[(2 + f) * Q : (3 + f) * Q].astype(bf16)
                power = jnp.mean(value * value, axis=1, keepdims=True)
                half = value * (lax.rsqrt(power + norm_eps) * mask) * half_gain
                active = half * jnp.tanh(half) + half
                a0, a1, a2, a3 = [active[f * Q : (f + 1) * Q] for f in range(4)]
                sides.append((a0 - a2, a1 + a2, a2 - a1, a1 - a3))
            for k in range(4):
                even, odd = sides[0][k], sides[1][k]
                comps[4 * k, line] = (moved_down(odd) - odd).astype(bf16)
                comps[4 * k + 1, line] = (even + odd).astype(bf16)
                comps[4 * k + 2, line] = (odd - even).astype(bf16)
                comps[4 * k + 3, line] = (even - moved_up(even)).astype(bf16)
        return 0

    for p in range(4):
        patch_row(p, 0)

    def finish(f, b, n, middle):
        cols = slice(n * 256, (n + 1) * 256)
        for r in range(6):
            line = 4 * s - 1 + r
            held = jnp.where(jnp.logical_and(line >= 0, line < 4 * ns), 1.0, 0.0)
            value = (
                skip[f, b, r + 1, :, cols].astype(f32)
                + middle[r * Q : (r + 1) * Q]
                + bias_mid[:, cols]
            ) * held
            rounded = value.astype(bf16)
            fine[f, r, b, :, cols] = rounded
            if b == 1:
                odd, even = rounded.astype(f32), fine[f, r, 0, :, cols].astype(f32)
                fine[f, r, 2, :, cols] = (even - moved_down(odd)).astype(bf16)
                fine[f, r, 3, :, cols] = (odd - even).astype(bf16)
                fine[f, r, 4, :, cols] = (moved_up(even) - odd).astype(bf16)

    def phase_weights(a):
        both = (wu.at[1], wu.at[2]) if a == 0 else (wu.at[0], wu.at[1])
        alone = wu.at[2 * a]
        wrow[...] = both[0][...] + both[1][...]
        for i in range(2):
            held = alone if i == a else wrow
            k0, k1, k2 = [held[k * CH : (k + 1) * CH] for k in range(3)]
            for n, value in enumerate((k0, k0 + k1 + k2, k2)):
                wphase[a, n, i] = value

    for k in range(4):
        if k == 0:
            mids[0].wait()
        if k == 1:
            mids[1].wait()
            mids[2].wait()
            up_load.wait()
        if k > 1:
            phase_weights(k - 2)
        source = wm.at[0] if k == 0 else wm.at[2] if k == 3 else staged
        if k in (1, 2):
            for j in range(3):
                ends = wm[0, j] + wm[2, j]
                staged[j] = ends + wm[1, j] if k == 1 else ends - wm[1, j]
        for j in range(3):
            left, centre, right = [source[j, c * CH : (c + 1) * CH] for c in range(3)]
            mixed[0, j * CH : (j + 1) * CH] = left + right + centre
            mixed[1, j * CH : (j + 1) * CH] = left + right - centre
        for n in range(2):
            cols = slice(n * 256, (n + 1) * 256)
            products = []
            for c in range(4):
                lhs = jnp.concatenate(
                    [comps[4 * k + c, j : j + 6].reshape(6 * Q, CH) for j in range(3)], axis=1
                )
                if c in (1, 2):
                    rhs = mixed[c - 1, :, cols]
                else:
                    at = 0 if c == 0 else 2 * CH
                    rhs = jnp.concatenate(
                        [source[j, at : at + CH, cols] for j in range(3)], axis=0
                    )
                products.append(jnp.dot(lhs, rhs, preferred_element_type=f32))
            m0, m1, m2, m3 = products
            for b, total in enumerate((m0 + 0.5 * (m1 + m2), 0.5 * (m1 - m2) - m3)):
                if k == 0:
                    pending[0, b, :, cols] = total
                elif k == 1:
                    pending[1, b, :, cols] = total
                elif k == 2:
                    held = pending[1, b, :, cols]
                    pending[1, b, :, cols] = 0.5 * (held - total)
                    finish(0, b, n, pending[0, b, :, cols] + 0.5 * (held + total))
                else:
                    finish(1, b, n, pending[1, b, :, cols] - total)

    writes = []

    def write_lines(f, a):
        for r in range(4):
            line = 8 * a + 4 * f + r
            for g in range(4):
                comps[line, 0:4, :, g * 128 : (g + 1) * 128] = stage[f, r, g].astype(bf16).reshape(
                    4, Q, 128
                )
            write = pltpu.make_async_copy(
                comps.at[line, 0:4], out_ref.at[f, r, a], osem.at[line]
            )
            write.start()
            writes.append(write)

    behind = None
    for a in range(2):
        for f in range(2):
            for n in range(2):
                cols = slice(n * 256, (n + 1) * 256)
                products = []
                for kind, at in enumerate((2, 0, 3)):
                    lhs = jnp.concatenate(
                        [
                            fine[f, a + i : a + i + 4, at : at + 2].reshape(8 * Q, CH)
                            for i in range(2)
                        ],
                        axis=1,
                    )
                    rhs = wphase[a, kind, :, :, cols].reshape(2 * CH, 256)
                    products.append(jnp.dot(lhs, rhs, preferred_element_type=f32))
                first, centre, last = products
                centre = centre + bias_up[:, cols]
                for b, value in enumerate((centre - first, centre + last)):
                    for r in range(4):
                        for side in range(2):
                            at = (2 * r + side) * Q
                            for g in range(2):
                                stage[f, r, 2 * n + g, pl.ds(2 * side + b, Q, stride=4), :] = value[
                                    at : at + Q, g * 128 : (g + 1) * 128
                                ]
            if behind is not None:
                write_lines(*behind)
            behind = (f, a)
    write_lines(*behind)
    for write in writes:
        write.wait()


def on_device(
    hidden, modulation, w_proj, b_proj, guidance, x_noisy, sigma, w_in, b_in, gain,
    w_mid, b_mid, w_up, b_up,
):
    vmem = pl.BlockSpec(memory_space=pltpu.VMEM)
    anywhere = pl.BlockSpec(memory_space=pltpu.HBM)
    rows = lambda v: v.reshape(1, -1)
    dma = pltpu.SemaphoreType.DMA
    windows = pl.pallas_call(
        latent_kernel,
        out_shape=jax.ShapeDtypeStruct((4, 6, Q, 256), bf16),
        in_specs=[anywhere] * 7,
        out_specs=vmem,
        scratch_shapes=[
            pltpu.VMEM((8 * Q + 16, 4096), bf16),
            pltpu.VMEM((64, 4096), bf16),
            pltpu.VMEM((2, 4096), f32),
            pltpu.VMEM((128, 4096), bf16),
            pltpu.VMEM((1, 64), f32),
            pltpu.VMEM((2, 1, 1), f32),
            pltpu.VMEM((2, 2, 2, 16, 128), f32),
            pltpu.VMEM((128, 128), f32),
            pltpu.VMEM((2, Q, 128), bf16),
            pltpu.VMEM((6, 3, Q, 128), bf16),
            pltpu.VMEM((6, 2, Q, 256), bf16),
            dma((8,)), dma((5,)), dma, dma, dma, dma((5,)), dma((6,)),
        ],
        compiler_params=pltpu.CompilerParams(
            collective_id=0, has_side_effects=True, vmem_limit_bytes=60 << 20
        ),
    )(
        hidden, modulation, w_proj.T, rows(b_proj), rows(guidance), rows(sigma),
        jnp.swapaxes(x_noisy, 2, 3),
    )
    decoded = pl.pallas_call(
        decoder_kernel,
        out_shape=jax.ShapeDtypeStruct((2, 4, 2, 4, Q, CH), bf16),
        in_specs=[anywhere] * 8,
        out_specs=anywhere,
        scratch_shapes=[
            pltpu.VMEM((4, 6, Q, 256), bf16),
            pltpu.VMEM((3, 3, 48, CH), bf16),
            pltpu.VMEM((768, 4 * CH), bf16),
            pltpu.VMEM((4, 1, CH), f32),
            pltpu.VMEM((3, 3, 3 * CH, CH), bf16),
            pltpu.VMEM((3, 3 * CH, CH), bf16),
            pltpu.VMEM((16, 8, Q, CH), bf16),
            pltpu.VMEM((2, 2, 8, Q, CH), bf16),
            pltpu.VMEM((3, 3 * CH, CH), bf16),
            pltpu.VMEM((2, 3 * CH, CH), bf16),
            pltpu.VMEM((2, 2, 6 * Q, CH), f32),
            pltpu.VMEM((2, 6, 5, Q, CH), bf16),
            pltpu.VMEM((3 * CH, CH), bf16),
            pltpu.VMEM((2, 3, 2, CH, CH), bf16),
            pltpu.VMEM((2, 4, 4, 256, 128), f32),
            dma, dma, dma((4,)), dma((3,)), dma, dma((16,)),
        ],
        compiler_params=pltpu.CompilerParams(vmem_limit_bytes=62 << 20),
    )(windows, w_in, rows(b_in), rows(gain), w_mid, rows(b_mid), w_up, rows(b_up))
    return decoded.reshape(2, 8, 256, CH)


def solution(mesh):
    return jax.shard_map(
        on_device,
        mesh=mesh,
        in_specs=(
            P(None, None, ("space", "tm"), None), P(), P(), P(), P(),
            P("tm", "space", None, None), P(), P(), P(), P(), P(), P(), P(), P(),
        ),
        out_specs=P("tm", "space", None, None),
        check_vma=False,
    )
```

```python
import functools

import jax
import jax.numpy as jnp
from jax import lax
from jax.experimental import pallas as pl
from jax.experimental.pallas import tpu as pltpu
from jax.sharding import PartitionSpec as P

MESH = pl.DeviceIdType.MESH
norm_eps = 1e-06
bf16, f32 = jnp.bfloat16, jnp.float32
CH = 512
Q = 64
NT = (((1,), (1,)), ((), ()))


def moved_down(x):
    at = lax.broadcasted_iota(jnp.int32, x.shape, 0)
    return jnp.where(at == 0, 0.0, pltpu.roll(x, 1, 0))


def moved_up(x):
    at = lax.broadcasted_iota(jnp.int32, x.shape, 0)
    return jnp.where(at == x.shape[0] - 1, 0.0, pltpu.roll(x, x.shape[0] - 1, 0))


def latent_kernel(
    h_ref, mod_ref, w_ref, b_ref, g_ref, sigma_ref, x_ref, windows,
    hbuf, wbuf, mod, wmat, bias_in, scalars, xall, xt, lat, land, wide,
    hsem, ssmall, xlocal, xsend, xrecv, ssem, rsem,
):
    s, t = lax.axis_index("space"), lax.axis_index("tm")
    ns = lax.axis_size("space")
    other = 1 - t
    after, before = s + 1, s - 1

    small = []
    for n, (a, b) in enumerate(
        ((w_ref, wbuf), (mod_ref, mod), (b_ref, bias_in), (g_ref, scalars.at[0]), (sigma_ref, scalars.at[1]))
    ):
        load = pltpu.make_async_copy(a, b, ssmall.at[n])
        load.start()
        small.append(load)
    loads = []
    for f in range(4):
        for k in range(2):
            load = pltpu.make_async_copy(
                h_ref.at[k, f], hbuf.at[(2 * f + k) * Q : (2 * f + k + 1) * Q], hsem.at[2 * f + k]
            )
            load.start()
            loads.append(load)
    x_load = pltpu.make_async_copy(x_ref.at[:, pl.ds(2 * t, 2)], xall.at[t], xlocal)
    x_load.start()

    land[...] = jnp.zeros(land.shape, bf16)
    barrier = pltpu.get_barrier_semaphore()
    pl.semaphore_signal(barrier, inc=1, device_id=(s, other), device_id_type=MESH)
    for held, row in ((s > 0, before), (s < ns - 1, after)):
        @pl.when(held)
        def _():
            for k in range(2):
                pl.semaphore_signal(barrier, inc=1, device_id=(row, k), device_id_type=MESH)

    pl.semaphore_wait(
        barrier, 1 + 2 * (s > 0).astype(jnp.int32) + 2 * (s < ns - 1).astype(jnp.int32)
    )
    x_copy = pltpu.make_async_remote_copy(
        src_ref=x_ref.at[:, pl.ds(2 * other, 2)], dst_ref=xall.at[t], send_sem=xsend,
        recv_sem=xrecv, device_id=(s, other), device_id_type=MESH,
    )
    x_copy.start()

    for load in small:
        load.wait()
    scale, shift = 1.0 + mod[1:2, :], mod[0:1, :]
    scaled_sum, shift_sum = jnp.zeros((Q, 128), f32), jnp.zeros((Q, 128), f32)
    for k in range(32):
        at = slice(k * 128, (k + 1) * 128)
        plain = jnp.concatenate(
            [wbuf[n * 16 : n * 16 + 16, at].astype(f32) for n in (0, 2, 1, 3)], axis=0
        )
        scaled = (plain * scale[:, at]).astype(bf16)
        wmat[:, at] = scaled
        scaled_sum = scaled_sum + scaled.astype(f32)
        shift_sum = shift_sum + plain * shift[:, at]
    totals = jnp.sum(
        jnp.transpose(jnp.concatenate([scaled_sum, shift_sum], axis=0)), axis=0, keepdims=True
    )
    bias = jnp.concatenate(
        [bias_in[:, n * 16 : n * 16 + 16] for n in (0, 2, 1, 3)], axis=1
    )
    column_sum, constant = totals[:, :Q], totals[:, Q:] + bias
    guidance, sigma = scalars[0], scalars[1]

    for load in loads:
        load.wait()
    product = lax.dot_general(hbuf[...], wmat[...], NT, preferred_element_type=f32)
    statistics = []
    for f in range(4):
        rows = hbuf[2 * f * Q : 2 * (f + 1) * Q]
        pivot = rows[:, 0:1].astype(f32)
        first, second = jnp.zeros((2 * Q, 128), f32), jnp.zeros((2 * Q, 128), f32)
        for k in range(32):
            part = rows[:, k * 128 : (k + 1) * 128].astype(f32) - pivot
            first = first + part
            second = second + part * part
        offset = jnp.sum(first, axis=1, keepdims=True) * (1.0 / 4096)
        spread = jnp.sum(second, axis=1, keepdims=True) * (1.0 / 4096) - offset * offset
        statistics.append((pivot + offset, lax.rsqrt(jnp.maximum(spread, 0.0) + norm_eps)))
    predictions = []
    for f in range(4):
        centre, inverse = statistics[f]
        branch = inverse * (product[2 * f * Q : 2 * (f + 1) * Q] - centre * column_sum)
        cond, uncond = branch[:Q], branch[Q:]
        predictions.append(uncond + guidance * (cond - uncond) + constant)

    x_load.wait()
    x_copy.wait()
    xt[...] = jnp.transpose(xall[...].reshape(128, 128))
    even, odd = xt[pl.ds(0, Q, stride=2), :], xt[pl.ds(1, Q, stride=2), :]
    for pair in range(2):
        latents = []
        for f in (2 * pair, 2 * pair + 1):
            at = slice(32 * f, 32 * f + 32)
            noisy = jnp.concatenate([even[:, at], odd[:, at]], axis=1)
            latents.append(noisy - sigma * predictions[f])
        lat[pair] = jnp.concatenate(latents, axis=1).astype(bf16)

    def send(peer, to, slot, k):
        count = 1 + to
        return pltpu.make_async_remote_copy(
            src_ref=lat.at[pl.ds(0, count)], dst_ref=land.at[slot, pl.ds(3 - count, count)],
            send_sem=ssem.at[k], recv_sem=rsem.at[slot], device_id=peer, device_id_type=MESH,
        )

    def send_row(row, slot, k):
        return [send((row, 1), 1, slot, k), send((row, 0), 0, slot, k + 1)]

    rows_held = ((s > 0, before, 4 + t, 0), (s < ns - 1, after, t, 2))
    for held, row, slot, k in rows_held:
        @pl.when(held)
        def _():
            for copy in send_row(row, slot, k):
                copy.start()
    for to in range(2):
        @pl.when(other == to)
        def _():
            send((s, to), to, 3 - to, 4).start()

    at = lax.broadcasted_iota(jnp.int32, (256, 256), 0)
    to = lax.broadcasted_iota(jnp.int32, (256, 256), 1)
    turn = (to // 16 + 3) % 4
    source = (turn // 2) * 128 + (to // 128) * 64 + (turn % 2) * 32 + ((to // 64) % 2) * 16 + to % 16
    widen = (at == source).astype(f32).astype(bf16)

    for me in range(2):
        @pl.when(t == me)
        def _():
            count = 1 + me
            land[2 + me, 3 - count : 3] = lat[0:count]
            send((s, other), me, 3 - me, 4).wait_recv()
            send((s, other), 1 - me, 2 + me, 4).wait_send()
            for held, slots in ((s > 0, (0, 1)), (s < ns - 1, (4, 5))):
                @pl.when(held)
                def _():
                    for slot in slots:
                        send((s, other), me, slot, 4).wait_recv()
    for held, row, slot, k in rows_held:
        @pl.when(held)
        def _():
            for copy in send_row(row, slot, k):
                copy.wait_send()

    position = lax.broadcasted_iota(jnp.int32, (Q, 128), 0)
    wide_lane = lax.broadcasted_iota(jnp.int32, (Q, 128), 1)
    parts = []
    for p in range(6):
        for pair in (1, 2):
            here = land[p, pair].astype(f32)
            from_left = jnp.where(position == 0, 0.0, pltpu.roll(here, 1, 0))
            from_right = jnp.where(position == Q - 1, 0.0, pltpu.roll(here, Q - 1, 0))
            beside = jnp.where((wide_lane // 32) % 2 == 0, from_right, from_left)
            parts.append(jnp.concatenate([here, beside], axis=1).astype(bf16))
    wide[...] = jnp.dot(
        jnp.concatenate(parts, axis=0), widen, preferred_element_type=f32
    ).astype(bf16).reshape(6, 2, Q, 256)
    for p in range(4):
        for f in range(2, 6):
            at = slice(f % 2 * 128, f % 2 * 128 + 128)
            above, own, below = [wide[p + k, f // 2 - 1, :, at] for k in range(3)]
            beside = jnp.where(wide_lane < 64, below.astype(f32), above.astype(f32)).astype(bf16)
            windows[p, f - 2] = jnp.concatenate([own, beside], axis=1)


def decoder_kernel(
    windows_ref, win_ref, bin_ref, gain_ref, wmid_ref, bmid_ref, wup_ref, bup_ref, out_ref,
    windows, win, wp, vectors, wm, wu, comps, skip, turned, mixed, last, pending, fine, wphase, stage, lsem, wsem, vsem, msem, usem, osem,
):
    s, t = lax.axis_index("space"), lax.axis_index("tm")
    ns = lax.axis_size("space")
    others = [
        pltpu.make_async_copy(windows_ref, windows.at[:, 2:6], lsem),
        pltpu.make_async_copy(win_ref, win, wsem),
    ]
    for n, ref in enumerate((bin_ref, gain_ref, bmid_ref, bup_ref)):
        others.append(pltpu.make_async_copy(ref, vectors.at[n], vsem.at[n]))
    for load in others:
        load.start()

    wp[...] = jnp.zeros(wp.shape, bf16)
    windows[:, 0:2] = jnp.zeros((4, 2, Q, 256), bf16)
    for n in range(2):
        for k in range(4):
            for b in range(2):
                turned[n, k, b, 0:8] = jnp.zeros((8, CH), f32)
                turned[n, k, b, 8 + Q :] = jnp.zeros((8, CH), f32)
    for load in others:
        load.wait()
    mids = [pltpu.make_async_copy(wmid_ref.at[i], wm.at[i], msem.at[i]) for i in range(3)]
    up_load = pltpu.make_async_copy(wup_ref, wu, usem)
    for load in mids + [up_load]:
        load.start()
    for i in range(3):
        for j in range(3):
            block = win[i, j]
            for a in range(2):
                for b in range(2):
                    at = i * 256 + ((a + j - 1) % 4) * 64 + b * 16
                    wp[at : at + 48, (2 * a + b) * CH : (2 * a + b + 1) * CH] = block

    bias_first, half_gain = vectors[0], 0.5 * vectors[1]
    bias_mid, bias_up = vectors[2], vectors[3]
    for p in range(4):
        lhs = jnp.concatenate(
            [windows[p, i : i + 4].reshape(4 * Q, 256) for i in range(3)], axis=1
        )
        for a in range(2):
            line = 2 * p + a
            held = jnp.logical_and(4 * s - 2 + line >= 0, 4 * s - 2 + line < 4 * ns)
            own = jnp.where(held, 1.0, 0.0)
            earlier = jnp.where(jnp.logical_and(held, t > 0), 1.0, 0.0)
            for b in range(2):
                column = (2 * a + b) * CH
                raw = jnp.dot(lhs, wp[:, column : column + CH], preferred_element_type=f32)
                for q in range(0, Q, 16):
                    active = []
                    for f in range(4):
                        value = raw[f * Q + q : f * Q + q + 16] + bias_first
                        if f >= 2:
                            skip[f - 2, b, line, q : q + 16] = value.astype(bf16)
                        power = jnp.mean(value * value, axis=1, keepdims=True)
                        factor = lax.rsqrt(power + norm_eps) * (earlier if f < 2 else own)
                        half = value * factor * half_gain
                        active.append(half * jnp.tanh(half) + half)
                    a0, a1, a2, a3 = active
                    for k, value in enumerate((a0 - a2, a1 + a2, a2 - a1, a1 - a3)):
                        turned[a, k, b, 8 + q : 24 + q] = value
            for k in range(4):
                for q in range(0, Q, 16):
                    even, odd = turned[a, k, 0, 8 + q : 24 + q], turned[a, k, 1, 8 + q : 24 + q]
                    before, after = turned[a, k, 1, 7 + q : 23 + q], turned[a, k, 0, 9 + q : 25 + q]
                    for c, value in enumerate((before - odd, even + odd, odd - even, even - after)):
                        comps[4 * k + c, line, q : q + 16] = value.astype(bf16)

    def finish(f, b, n, middle):
        cols = slice(n * 256, (n + 1) * 256)
        for r in range(6):
            line = 4 * s - 1 + r
            held = jnp.where(jnp.logical_and(line >= 0, line < 4 * ns), 1.0, 0.0)
            value = (
                skip[f, b, r + 1, :, cols].astype(f32)
                + middle[r * Q : (r + 1) * Q]
                + bias_mid[:, cols]
            ) * held
            rounded = value.astype(bf16)
            fine[f, r, b, :, cols] = rounded
            if b == 1:
                odd, even = rounded.astype(f32), fine[f, r, 0, :, cols].astype(f32)
                fine[f, r, 2, :, cols] = (even - moved_down(odd)).astype(bf16)
                fine[f, r, 3, :, cols] = (odd - even).astype(bf16)
                fine[f, r, 4, :, cols] = (moved_up(even) - odd).astype(bf16)

    def rows_of(ref, at):
        return ref[at : at + 16].astype(f32)

    def mix_outer(i, slot):
        for j in range(3):
            for r in range(0, CH, 16):
                left, centre, right = [rows_of(wm.at[i, j], m * CH + r) for m in range(3)]
                ends = left + right
                mixed[slot, 0, j * CH + r : j * CH + r + 16] = (ends + centre).astype(bf16)
                mixed[slot, 1, j * CH + r : j * CH + r + 16] = (ends - centre).astype(bf16)

    places = {
        (1, 0): (0, 0), (1, 1): (0, 1), (1, 2): (0, 2), (1, 3): (1, 0),
        (2, 0): (1, 1), (2, 1): (1, 2), (2, 2): (2, 1),
    }

    def mix_inner():
        for j in range(3):
            for r in range(0, CH, 16):
                taps = [[rows_of(wm.at[i, j], m * CH + r) for m in range(3)] for i in range(3)]
                sums, differences = [], []
                for m in range(3):
                    ends = taps[0][m] + taps[2][m]
                    sums.append(ends + taps[1][m])
                    differences.append(ends - taps[1][m])
                for k, (left, centre, right) in ((1, sums), (2, differences)):
                    ends = left + right
                    for c, value in enumerate((left, ends + centre, ends - centre, right)):
                        if (k, c) in places:
                            i, m = places[k, c]
                            wm[i, j, m * CH + r : m * CH + r + 16] = value.astype(bf16)
                        else:
                            last[j * CH + r : j * CH + r + 16] = value.astype(bf16)

    def phase_weights(start):
        for r in range(start, start + CH // 2, 16):
            taps = [[rows_of(wu.at[j], m * CH + r) for m in range(3)] for j in range(3)]
            low = [taps[0][m] + taps[1][m] for m in range(3)]
            high = [taps[1][m] + taps[2][m] for m in range(3)]
            for a, i, (left, centre, right) in (
                (0, 0, taps[0]), (0, 1, high), (1, 0, low), (1, 1, taps[2])
            ):
                for n, value in enumerate((left, left + centre + right, right)):
                    wphase[a, n, i, r : r + 16] = value.astype(bf16)

    def middle_weights(k, c, cols):
        if k in (0, 3) and c in (1, 2):
            return mixed[k // 3, c - 1, :, cols]
        if (k, c) == (2, 3):
            return last[:, cols]
        i, m = places[k, c] if k in (1, 2) else (2 * (k // 3), 2 * (c // 3))
        return wm[i, :, m * CH : (m + 1) * CH, cols].reshape(3 * CH, 256)

    for load in mids:
        load.wait()
    mix_outer(0, 0)
    mix_outer(2, 1)
    for k in (0, 3, 1, 2):
        if k == 3:
            mix_inner()
        if k == 1:
            up_load.wait()
            phase_weights(0)
        if k == 2:
            phase_weights(CH // 2)
        for n in range(2):
            cols = slice(n * 256, (n + 1) * 256)
            products = []
            for c in range(4):
                lhs = jnp.concatenate(
                    [comps[4 * k + c, j : j + 6].reshape(6 * Q, CH) for j in range(3)], axis=1
                )
                products.append(
                    jnp.dot(lhs, middle_weights(k, c, cols), preferred_element_type=f32)
                )
            m0, m1, m2, m3 = products
            for b, total in enumerate((m0 + 0.5 * (m1 + m2), 0.5 * (m1 - m2) - m3)):
                if k in (0, 3):
                    pending[k // 3, b, :, cols] = total
                elif k == 1:
                    pending[0, b, :, cols] = pending[0, b, :, cols] + 0.5 * total
                    pending[1, b, :, cols] = 0.5 * total - pending[1, b, :, cols]
                else:
                    finish(0, b, n, pending[0, b, :, cols] + 0.5 * total)
                    finish(1, b, n, pending[1, b, :, cols] - 0.5 * total)

    writes = []

    def write_lines(f, a):
        for r in range(4):
            line = 8 * a + 4 * f + r
            for g in range(4):
                comps[line, 0:4, :, g * 128 : (g + 1) * 128] = stage[f, r, g].astype(bf16).reshape(
                    4, Q, 128
                )
            write = pltpu.make_async_copy(
                comps.at[line, 0:4], out_ref.at[f, r, a], osem.at[line]
            )
            write.start()
            writes.append(write)

    behind = None
    for a in range(2):
        for f in range(2):
            for n in range(2):
                cols = slice(n * 256, (n + 1) * 256)
                products = []
                for kind, at in enumerate((2, 0, 3)):
                    lhs = jnp.concatenate(
                        [
                            fine[f, a + i : a + i + 4, at : at + 2].reshape(8 * Q, CH)
                            for i in range(2)
                        ],
                        axis=1,
                    )
                    rhs = wphase[a, kind, :, :, cols].reshape(2 * CH, 256)
                    products.append(jnp.dot(lhs, rhs, preferred_element_type=f32))
                first, centre, last = products
                centre = centre + bias_up[:, cols]
                for b, value in enumerate((centre - first, centre + last)):
                    for r in range(4):
                        for side in range(2):
                            at = (2 * r + side) * Q
                            for g in range(2):
                                stage[f, r, 2 * n + g, pl.ds(2 * side + b, Q, stride=4), :] = value[
                                    at : at + Q, g * 128 : (g + 1) * 128
                                ]
            if behind is not None:
                write_lines(*behind)
            behind = (f, a)
    write_lines(*behind)
    for write in writes:
        write.wait()


def on_device(
    hidden, modulation, w_proj, b_proj, guidance, x_noisy, sigma, w_in, b_in, gain,
    w_mid, b_mid, w_up, b_up,
):
    vmem = pl.BlockSpec(memory_space=pltpu.VMEM)
    anywhere = pl.BlockSpec(memory_space=pltpu.HBM)
    rows = lambda v: v.reshape(1, -1)
    dma = pltpu.SemaphoreType.DMA
    windows = pl.pallas_call(
        latent_kernel,
        out_shape=jax.ShapeDtypeStruct((4, 4, Q, 256), bf16),
        in_specs=[anywhere] * 7,
        out_specs=vmem,
        scratch_shapes=[
            pltpu.VMEM((8 * Q, 4096), bf16),
            pltpu.VMEM((64, 4096), bf16),
            pltpu.VMEM((2, 4096), f32),
            pltpu.VMEM((64, 4096), bf16),
            pltpu.VMEM((1, 64), f32),
            pltpu.VMEM((2, 1, 1), f32),
            pltpu.VMEM((2, 2, 2, 16, 128), f32),
            pltpu.VMEM((128, 128), f32),
            pltpu.VMEM((2, Q, 128), bf16),
            pltpu.VMEM((6, 3, Q, 128), bf16),
            pltpu.VMEM((6, 2, Q, 256), bf16),
            dma((8,)), dma((5,)), dma, dma, dma, dma((5,)), dma((6,)),
        ],
        compiler_params=pltpu.CompilerParams(
            collective_id=0, has_side_effects=True, vmem_limit_bytes=60 << 20
        ),
    )(
        hidden, modulation, w_proj.T, rows(b_proj), rows(guidance), rows(sigma),
        jnp.swapaxes(x_noisy, 2, 3),
    )
    decoded = pl.pallas_call(
        decoder_kernel,
        out_shape=jax.ShapeDtypeStruct((2, 4, 2, 4, Q, CH), bf16),
        in_specs=[anywhere] * 8,
        out_specs=anywhere,
        scratch_shapes=[
            pltpu.VMEM((4, 6, Q, 256), bf16),
            pltpu.VMEM((3, 3, 48, CH), bf16),
            pltpu.VMEM((768, 4 * CH), bf16),
            pltpu.VMEM((4, 1, CH), f32),
            pltpu.VMEM((3, 3, 3 * CH, CH), bf16),
            pltpu.VMEM((3, 3 * CH, CH), bf16),
            pltpu.VMEM((16, 8, Q, CH), bf16),
            pltpu.VMEM((2, 2, 8, Q, CH), bf16),
            pltpu.VMEM((2, 4, 2, Q + 16, CH), f32),
            pltpu.VMEM((2, 2, 3 * CH, CH), bf16),
            pltpu.VMEM((3 * CH, CH), bf16),
            pltpu.VMEM((2, 2, 6 * Q, CH), f32),
            pltpu.VMEM((2, 6, 5, Q, CH), bf16),
            pltpu.VMEM((2, 3, 2, CH, CH), bf16),
            pltpu.VMEM((2, 4, 4, 256, 128), f32),
            dma, dma, dma((4,)), dma((3,)), dma, dma((16,)),
        ],
        compiler_params=pltpu.CompilerParams(vmem_limit_bytes=62 << 20),
    )(windows, w_in, rows(b_in), rows(gain), w_mid, rows(b_mid), w_up, rows(b_up))
    return decoded.reshape(2, 8, 256, CH)


def solution(mesh):
    return jax.shard_map(
        on_device,
        mesh=mesh,
        in_specs=(
            P(None, None, ("space", "tm"), None), P(), P(), P(), P(),
            P("tm", "space", None, None), P(), P(), P(), P(), P(), P(), P(), P(),
        ),
        out_specs=P("tm", "space", None, None),
        check_vma=False,
    )
```

```python
import functools

import jax
import jax.numpy as jnp
from jax import lax
from jax.experimental import pallas as pl
from jax.experimental.pallas import tpu as pltpu
from jax.sharding import PartitionSpec as P

MESH = pl.DeviceIdType.MESH
norm_eps = 1e-06
bf16, f32 = jnp.bfloat16, jnp.float32
CH = 512
Q = 64
NT = (((1,), (1,)), ((), ()))


def moved_down(x):
    at = lax.broadcasted_iota(jnp.int32, x.shape, 0)
    return jnp.where(at == 0, 0.0, pltpu.roll(x, 1, 0))


def moved_up(x):
    at = lax.broadcasted_iota(jnp.int32, x.shape, 0)
    return jnp.where(at == x.shape[0] - 1, 0.0, pltpu.roll(x, x.shape[0] - 1, 0))


def latent_kernel(
    h_ref, mod_ref, w_ref, b_ref, g_ref, sigma_ref, x_ref, windows,
    hbuf, wbuf, mod, wmat, bias_in, scalars, xall, xt, lat, land, wide,
    hsem, ssmall, xlocal, xsend, xrecv, ssem, rsem,
):
    s, t = lax.axis_index("space"), lax.axis_index("tm")
    ns = lax.axis_size("space")
    other = 1 - t
    after, before = s + 1, s - 1

    small = []
    for n, (a, b) in enumerate(
        ((w_ref, wbuf), (mod_ref, mod), (b_ref, bias_in), (g_ref, scalars.at[0]), (sigma_ref, scalars.at[1]))
    ):
        load = pltpu.make_async_copy(a, b, ssmall.at[n])
        load.start()
        small.append(load)
    loads = []
    for f in range(4):
        for k in range(2):
            load = pltpu.make_async_copy(
                h_ref.at[k, f], hbuf.at[(2 * f + k) * Q : (2 * f + k + 1) * Q], hsem.at[2 * f + k]
            )
            load.start()
            loads.append(load)
    x_load = pltpu.make_async_copy(x_ref.at[:, pl.ds(2 * t, 2)], xall.at[t], xlocal)
    x_load.start()

    land[...] = jnp.zeros(land.shape, bf16)
    barrier = pltpu.get_barrier_semaphore()
    pl.semaphore_signal(barrier, inc=1, device_id=(s, other), device_id_type=MESH)
    for held, row in ((s > 0, before), (s < ns - 1, after)):
        @pl.when(held)
        def _():
            for k in range(2):
                pl.semaphore_signal(barrier, inc=1, device_id=(row, k), device_id_type=MESH)

    pl.semaphore_wait(
        barrier, 1 + 2 * (s > 0).astype(jnp.int32) + 2 * (s < ns - 1).astype(jnp.int32)
    )
    x_copy = pltpu.make_async_remote_copy(
        src_ref=x_ref.at[:, pl.ds(2 * other, 2)], dst_ref=xall.at[t], send_sem=xsend,
        recv_sem=xrecv, device_id=(s, other), device_id_type=MESH,
    )
    x_copy.start()

    for load in small:
        load.wait()
    scale, shift = 1.0 + mod[1:2, :], mod[0:1, :]
    scaled_sum, shift_sum = jnp.zeros((Q, 128), f32), jnp.zeros((Q, 128), f32)
    for k in range(32):
        at = slice(k * 128, (k + 1) * 128)
        plain = jnp.concatenate(
            [wbuf[n * 16 : n * 16 + 16, at].astype(f32) for n in (0, 2, 1, 3)], axis=0
        )
        scaled = (plain * scale[:, at]).astype(bf16)
        wmat[:, at] = scaled
        scaled_sum = scaled_sum + scaled.astype(f32)
        shift_sum = shift_sum + plain * shift[:, at]
    totals = jnp.sum(
        jnp.transpose(jnp.concatenate([scaled_sum, shift_sum], axis=0)), axis=0, keepdims=True
    )
    bias = jnp.concatenate(
        [bias_in[:, n * 16 : n * 16 + 16] for n in (0, 2, 1, 3)], axis=1
    )
    column_sum, constant = totals[:, :Q], totals[:, Q:] + bias
    guidance, sigma = scalars[0], scalars[1]

    for load in loads:
        load.wait()
    product = lax.dot_general(hbuf[...], wmat[...], NT, preferred_element_type=f32)
    statistics = []
    for f in range(4):
        rows = hbuf[2 * f * Q : 2 * (f + 1) * Q]
        pivot = rows[:, 0:1].astype(f32)
        first, second = jnp.zeros((2 * Q, 128), f32), jnp.zeros((2 * Q, 128), f32)
        for k in range(32):
            part = rows[:, k * 128 : (k + 1) * 128].astype(f32) - pivot
            first = first + part
            second = second + part * part
        offset = jnp.sum(first, axis=1, keepdims=True) * (1.0 / 4096)
        spread = jnp.sum(second, axis=1, keepdims=True) * (1.0 / 4096) - offset * offset
        statistics.append((pivot + offset, lax.rsqrt(jnp.maximum(spread, 0.0) + norm_eps)))
    predictions = []
    for f in range(4):
        centre, inverse = statistics[f]
        branch = inverse * (product[2 * f * Q : 2 * (f + 1) * Q] - centre * column_sum)
        cond, uncond = branch[:Q], branch[Q:]
        predictions.append(uncond + guidance * (cond - uncond) + constant)

    x_load.wait()
    x_copy.wait()
    xt[...] = jnp.transpose(xall[...].reshape(128, 128))
    even, odd = xt[pl.ds(0, Q, stride=2), :], xt[pl.ds(1, Q, stride=2), :]
    for pair in range(2):
        latents = []
        for f in (2 * pair, 2 * pair + 1):
            at = slice(32 * f, 32 * f + 32)
            noisy = jnp.concatenate([even[:, at], odd[:, at]], axis=1)
            latents.append(noisy - sigma * predictions[f])
        lat[pair] = jnp.concatenate(latents, axis=1).astype(bf16)

    def send(peer, to, slot, k):
        count = 1 + to
        return pltpu.make_async_remote_copy(
            src_ref=lat.at[pl.ds(0, count)], dst_ref=land.at[slot, pl.ds(3 - count, count)],
            send_sem=ssem.at[k], recv_sem=rsem.at[slot], device_id=peer, device_id_type=MESH,
        )

    def send_row(row, slot, k):
        return [send((row, 1), 1, slot, k), send((row, 0), 0, slot, k + 1)]

    rows_held = ((s > 0, before, 4 + t, 0), (s < ns - 1, after, t, 2))
    for held, row, slot, k in rows_held:
        @pl.when(held)
        def _():
            for copy in send_row(row, slot, k):
                copy.start()
    for to in range(2):
        @pl.when(other == to)
        def _():
            send((s, to), to, 3 - to, 4).start()

    at = lax.broadcasted_iota(jnp.int32, (256, 256), 0)
    to = lax.broadcasted_iota(jnp.int32, (256, 256), 1)
    turn = (to // 16 + 3) % 4
    source = (turn // 2) * 128 + (to // 128) * 64 + (turn % 2) * 32 + ((to // 64) % 2) * 16 + to % 16
    widen = (at == source).astype(f32).astype(bf16)

    for me in range(2):
        @pl.when(t == me)
        def _():
            count = 1 + me
            land[2 + me, 3 - count : 3] = lat[0:count]
            send((s, other), me, 3 - me, 4).wait_recv()
            send((s, other), 1 - me, 2 + me, 4).wait_send()
            for held, slots in ((s > 0, (0, 1)), (s < ns - 1, (4, 5))):
                @pl.when(held)
                def _():
                    for slot in slots:
                        send((s, other), me, slot, 4).wait_recv()
    for held, row, slot, k in rows_held:
        @pl.when(held)
        def _():
            for copy in send_row(row, slot, k):
                copy.wait_send()

    position = lax.broadcasted_iota(jnp.int32, (Q, 128), 0)
    wide_lane = lax.broadcasted_iota(jnp.int32, (Q, 128), 1)
    parts = []
    for p in range(6):
        for pair in (1, 2):
            here = land[p, pair].astype(f32)
            from_left = jnp.where(position == 0, 0.0, pltpu.roll(here, 1, 0))
            from_right = jnp.where(position == Q - 1, 0.0, pltpu.roll(here, Q - 1, 0))
            beside = jnp.where((wide_lane // 32) % 2 == 0, from_right, from_left)
            parts.append(jnp.concatenate([here, beside], axis=1).astype(bf16))
    wide[...] = jnp.dot(
        jnp.concatenate(parts, axis=0), widen, preferred_element_type=f32
    ).astype(bf16).reshape(6, 2, Q, 256)
    for p in range(4):
        for f in range(2, 6):
            at = slice(f % 2 * 128, f % 2 * 128 + 128)
            above, own, below = [wide[p + k, f // 2 - 1, :, at] for k in range(3)]
            beside = jnp.where(wide_lane < 64, below.astype(f32), above.astype(f32)).astype(bf16)
            windows[p, f - 2] = jnp.concatenate([own, beside], axis=1)


def decoder_kernel(
    windows_ref, win_ref, bin_ref, gain_ref, wmid_ref, bmid_ref, wup_ref, bup_ref, out_ref,
    windows, win, wp, vectors, wm, wu, comps, skip, turned, mixed, last, pending, fine, wphase, stage, lsem, wsem, vsem, msem, usem, osem,
):
    s, t = lax.axis_index("space"), lax.axis_index("tm")
    ns = lax.axis_size("space")
    others = [
        pltpu.make_async_copy(windows_ref, windows.at[:, 2:6], lsem),
        pltpu.make_async_copy(win_ref, win, wsem),
    ]
    for n, ref in enumerate((bin_ref, gain_ref, bmid_ref, bup_ref)):
        others.append(pltpu.make_async_copy(ref, vectors.at[n], vsem.at[n]))
    for load in others:
        load.start()

    wp[...] = jnp.zeros(wp.shape, bf16)
    windows[:, 0:2] = jnp.zeros((4, 2, Q, 256), bf16)
    for n in range(2):
        for k in range(4):
            for b in range(2):
                turned[n, k, b, 0:8] = jnp.zeros((8, CH), f32)
                turned[n, k, b, 8 + Q :] = jnp.zeros((8, CH), f32)
    for load in others:
        load.wait()
    mids = [pltpu.make_async_copy(wmid_ref.at[i], wm.at[i], msem.at[i]) for i in range(3)]
    up_load = pltpu.make_async_copy(wup_ref, wu, usem)
    for load in mids + [up_load]:
        load.start()
    for i in range(3):
        for j in range(3):
            block = win[i, j]
            for a in range(2):
                for b in range(2):
                    at = i * 256 + ((a + j - 1) % 4) * 64 + b * 16
                    wp[at : at + 48, (2 * a + b) * CH : (2 * a + b + 1) * CH] = block

    bias_first, half_gain = vectors[0], 0.5 * vectors[1]
    bias_mid, bias_up = vectors[2], vectors[3]
    for p in range(4):
        lhs = jnp.concatenate(
            [windows[p, i : i + 4].reshape(4 * Q, 256) for i in range(3)], axis=1
        )
        for a in range(2):
            line = 2 * p + a
            held = jnp.logical_and(4 * s - 2 + line >= 0, 4 * s - 2 + line < 4 * ns)
            own = jnp.where(held, 1.0, 0.0)
            earlier = jnp.where(jnp.logical_and(held, t > 0), 1.0, 0.0)
            for b in range(2):
                column = (2 * a + b) * CH
                raw = jnp.dot(lhs, wp[:, column : column + CH], preferred_element_type=f32)
                for q in range(0, Q, 16):
                    active = []
                    for f in range(4):
                        value = raw[f * Q + q : f * Q + q + 16] + bias_first
                        if f >= 2:
                            skip[f - 2, b, line, q : q + 16] = value.astype(bf16)
                        power = jnp.mean(value * value, axis=1, keepdims=True)
                        factor = lax.rsqrt(power + norm_eps) * (earlier if f < 2 else own)
                        half = value * factor * half_gain
                        active.append(half * jnp.tanh(half) + half)
                    a0, a1, a2, a3 = active
                    for k, value in enumerate((a0 - a2, a1 + a2, a2 - a1, a1 - a3)):
                        turned[a, k, b, 8 + q : 24 + q] = value
            for k in range(4):
                for q in range(0, Q, 16):
                    even, odd = turned[a, k, 0, 8 + q : 24 + q], turned[a, k, 1, 8 + q : 24 + q]
                    before, after = turned[a, k, 1, 7 + q : 23 + q], turned[a, k, 0, 9 + q : 25 + q]
                    for c, value in enumerate((before - odd, even + odd, odd - even, even - after)):
                        comps[4 * k + c, line, q : q + 16] = value.astype(bf16)

    def finish(f, b, n, middle):
        cols = slice(n * 256, (n + 1) * 256)
        for r in range(6):
            line = 4 * s - 1 + r
            held = jnp.where(jnp.logical_and(line >= 0, line < 4 * ns), 1.0, 0.0)
            value = (
                skip[f, b, r + 1, :, cols].astype(f32)
                + middle[r * Q : (r + 1) * Q]
                + bias_mid[:, cols]
            ) * held
            rounded = value.astype(bf16)
            fine[f, r, b, :, cols] = rounded
            if b == 1:
                odd, even = rounded.astype(f32), fine[f, r, 0, :, cols].astype(f32)
                fine[f, r, 2, :, cols] = (even - moved_down(odd)).astype(bf16)
                fine[f, r, 3, :, cols] = (odd - even).astype(bf16)
                fine[f, r, 4, :, cols] = (moved_up(even) - odd).astype(bf16)

    def rows_of(ref, at):
        return ref[at : at + 16]

    def mix_outer(i, slot):
        for j in range(3):
            for r in range(0, CH, 16):
                left, centre, right = [rows_of(wm.at[i, j], m * CH + r) for m in range(3)]
                ends = left + right
                mixed[slot, 0, j * CH + r : j * CH + r + 16] = ends + centre
                mixed[slot, 1, j * CH + r : j * CH + r + 16] = ends - centre

    places = {
        (1, 0): (0, 0), (1, 1): (0, 1), (1, 2): (0, 2), (1, 3): (1, 0),
        (2, 0): (1, 1), (2, 1): (1, 2), (2, 2): (2, 1),
    }

    def mix_inner():
        for j in range(3):
            for r in range(0, CH, 16):
                taps = [[rows_of(wm.at[i, j], m * CH + r) for m in range(3)] for i in range(3)]
                sums, differences = [], []
                for m in range(3):
                    ends = taps[0][m] + taps[2][m]
                    sums.append(ends + taps[1][m])
                    differences.append(ends - taps[1][m])
                for k, (left, centre, right) in ((1, sums), (2, differences)):
                    ends = left + right
                    for c, value in enumerate((left, ends + centre, ends - centre, right)):
                        if (k, c) in places:
                            i, m = places[k, c]
                            wm[i, j, m * CH + r : m * CH + r + 16] = value
                        else:
                            last[j * CH + r : j * CH + r + 16] = value

    def phase_weights(start):
        for r in range(start, start + CH // 2, 16):
            taps = [[rows_of(wu.at[j], m * CH + r) for m in range(3)] for j in range(3)]
            low = [taps[0][m] + taps[1][m] for m in range(3)]
            high = [taps[1][m] + taps[2][m] for m in range(3)]
            for a, i, (left, centre, right) in (
                (0, 0, taps[0]), (0, 1, high), (1, 0, low), (1, 1, taps[2])
            ):
                for n, value in enumerate((left, left + centre + right, right)):
                    wphase[a, n, i, r : r + 16] = value

    def middle_weights(k, c, cols):
        if k in (0, 3) and c in (1, 2):
            return mixed[k // 3, c - 1, :, cols]
        if (k, c) == (2, 3):
            return last[:, cols]
        i, m = places[k, c] if k in (1, 2) else (2 * (k // 3), 2 * (c // 3))
        return wm[i, :, m * CH : (m + 1) * CH, cols].reshape(3 * CH, 256)

    mids[0].wait()
    mix_outer(0, 0)
    for k in (0, 3, 1, 2):
        if k == 3:
            mids[1].wait()
            mids[2].wait()
            mix_outer(2, 1)
            mix_inner()
        if k == 1:
            up_load.wait()
            phase_weights(0)
        if k == 2:
            phase_weights(CH // 2)
        for n in range(2):
            cols = slice(n * 256, (n + 1) * 256)
            products = []
            for c in range(4):
                lhs = jnp.concatenate(
                    [comps[4 * k + c, j : j + 6].reshape(6 * Q, CH) for j in range(3)], axis=1
                )
                products.append(
                    jnp.dot(lhs, middle_weights(k, c, cols), preferred_element_type=f32)
                )
            m0, m1, m2, m3 = products
            for b, total in enumerate((m0 + 0.5 * (m1 + m2), 0.5 * (m1 - m2) - m3)):
                if k in (0, 3):
                    pending[k // 3, b, :, cols] = total
                elif k == 1:
                    pending[0, b, :, cols] = pending[0, b, :, cols] + 0.5 * total
                    pending[1, b, :, cols] = 0.5 * total - pending[1, b, :, cols]
                else:
                    finish(0, b, n, pending[0, b, :, cols] + 0.5 * total)
                    finish(1, b, n, pending[1, b, :, cols] - 0.5 * total)

    writes = []

    def write_lines(f, a):
        for r in range(4):
            line = 8 * a + 4 * f + r
            for g in range(4):
                comps[line, 0:4, :, g * 128 : (g + 1) * 128] = stage[f, r, g].astype(bf16).reshape(
                    4, Q, 128
                )
            write = pltpu.make_async_copy(
                comps.at[line, 0:4], out_ref.at[f, r, a], osem.at[line]
            )
            write.start()
            writes.append(write)

    behind = None
    for a in range(2):
        for f in range(2):
            for n in range(2):
                cols = slice(n * 256, (n + 1) * 256)
                products = []
                for kind, at in enumerate((2, 0, 3)):
                    lhs = jnp.concatenate(
                        [
                            fine[f, a + i : a + i + 4, at : at + 2].reshape(8 * Q, CH)
                            for i in range(2)
                        ],
                        axis=1,
                    )
                    rhs = wphase[a, kind, :, :, cols].reshape(2 * CH, 256)
                    products.append(jnp.dot(lhs, rhs, preferred_element_type=f32))
                first, centre, last = products
                centre = centre + bias_up[:, cols]
                for b, value in enumerate((centre - first, centre + last)):
                    for r in range(4):
                        for side in range(2):
                            at = (2 * r + side) * Q
                            for g in range(2):
                                stage[f, r, 2 * n + g, pl.ds(2 * side + b, Q, stride=4), :] = value[
                                    at : at + Q, g * 128 : (g + 1) * 128
                                ]
            if behind is not None:
                write_lines(*behind)
            behind = (f, a)
    write_lines(*behind)
    for write in writes:
        write.wait()


def on_device(
    hidden, modulation, w_proj, b_proj, guidance, x_noisy, sigma, w_in, b_in, gain,
    w_mid, b_mid, w_up, b_up,
):
    vmem = pl.BlockSpec(memory_space=pltpu.VMEM)
    anywhere = pl.BlockSpec(memory_space=pltpu.HBM)
    rows = lambda v: v.reshape(1, -1)
    dma = pltpu.SemaphoreType.DMA
    windows = pl.pallas_call(
        latent_kernel,
        out_shape=jax.ShapeDtypeStruct((4, 4, Q, 256), bf16),
        in_specs=[anywhere] * 7,
        out_specs=vmem,
        scratch_shapes=[
            pltpu.VMEM((8 * Q, 4096), bf16),
            pltpu.VMEM((64, 4096), bf16),
            pltpu.VMEM((2, 4096), f32),
            pltpu.VMEM((64, 4096), bf16),
            pltpu.VMEM((1, 64), f32),
            pltpu.VMEM((2, 1, 1), f32),
            pltpu.VMEM((2, 2, 2, 16, 128), f32),
            pltpu.VMEM((128, 128), f32),
            pltpu.VMEM((2, Q, 128), bf16),
            pltpu.VMEM((6, 3, Q, 128), bf16),
            pltpu.VMEM((6, 2, Q, 256), bf16),
            dma((8,)), dma((5,)), dma, dma, dma, dma((5,)), dma((6,)),
        ],
        compiler_params=pltpu.CompilerParams(
            collective_id=0, has_side_effects=True, vmem_limit_bytes=60 << 20
        ),
    )(
        hidden, modulation, w_proj.T, rows(b_proj), rows(guidance), rows(sigma),
        jnp.swapaxes(x_noisy, 2, 3),
    )
    decoded = pl.pallas_call(
        decoder_kernel,
        out_shape=jax.ShapeDtypeStruct((2, 4, 2, 4, Q, CH), bf16),
        in_specs=[anywhere] * 8,
        out_specs=anywhere,
        scratch_shapes=[
            pltpu.VMEM((4, 6, Q, 256), bf16),
            pltpu.VMEM((3, 3, 48, CH), bf16),
            pltpu.VMEM((768, 4 * CH), bf16),
            pltpu.VMEM((4, 1, CH), f32),
            pltpu.VMEM((3, 3, 3 * CH, CH), bf16),
            pltpu.VMEM((3, 3 * CH, CH), bf16),
            pltpu.VMEM((16, 8, Q, CH), bf16),
            pltpu.VMEM((2, 2, 8, Q, CH), bf16),
            pltpu.VMEM((2, 4, 2, Q + 16, CH), f32),
            pltpu.VMEM((2, 2, 3 * CH, CH), bf16),
            pltpu.VMEM((3 * CH, CH), bf16),
            pltpu.VMEM((2, 2, 6 * Q, CH), f32),
            pltpu.VMEM((2, 6, 5, Q, CH), bf16),
            pltpu.VMEM((2, 3, 2, CH, CH), bf16),
            pltpu.VMEM((2, 4, 4, 256, 128), f32),
            dma, dma, dma((4,)), dma((3,)), dma, dma((16,)),
        ],
        compiler_params=pltpu.CompilerParams(vmem_limit_bytes=62 << 20),
    )(windows, w_in, rows(b_in), rows(gain), w_mid, rows(b_mid), w_up, rows(b_up))
    return decoded.reshape(2, 8, 256, CH)


def solution(mesh):
    return jax.shard_map(
        on_device,
        mesh=mesh,
        in_specs=(
            P(None, None, ("space", "tm"), None), P(), P(), P(), P(),
            P("tm", "space", None, None), P(), P(), P(), P(), P(), P(), P(), P(),
        ),
        out_specs=P("tm", "space", None, None),
        check_vma=False,
    )
```

```python
import functools

import jax
import jax.numpy as jnp
from jax import lax
from jax.experimental import pallas as pl
from jax.experimental.pallas import tpu as pltpu
from jax.sharding import PartitionSpec as P

MESH = pl.DeviceIdType.MESH
norm_eps = 1e-06
bf16, f32 = jnp.bfloat16, jnp.float32
CH = 512
Q = 64
NT = (((1,), (1,)), ((), ()))


def moved_down(x):
    at = lax.broadcasted_iota(jnp.int32, x.shape, 0)
    return jnp.where(at == 0, 0.0, pltpu.roll(x, 1, 0))


def moved_up(x):
    at = lax.broadcasted_iota(jnp.int32, x.shape, 0)
    return jnp.where(at == x.shape[0] - 1, 0.0, pltpu.roll(x, x.shape[0] - 1, 0))


def latent_kernel(
    h_ref, mod_ref, w_ref, b_ref, g_ref, sigma_ref, x_ref, windows,
    hbuf, wbuf, mod, wmat, bias_in, scalars, xall, xt, lat, land, wide,
    hsem, ssmall, xlocal, xsend, xrecv, ssem, rsem,
):
    s, t = lax.axis_index("space"), lax.axis_index("tm")
    ns = lax.axis_size("space")
    other = 1 - t
    after, before = s + 1, s - 1

    small = []
    for n, (a, b) in enumerate(
        ((w_ref, wbuf), (mod_ref, mod), (b_ref, bias_in), (g_ref, scalars.at[0]), (sigma_ref, scalars.at[1]))
    ):
        load = pltpu.make_async_copy(a, b, ssmall.at[n])
        load.start()
        small.append(load)
    loads = []
    for f in range(4):
        for k in range(2):
            load = pltpu.make_async_copy(
                h_ref.at[k, f], hbuf.at[(2 * f + k) * Q : (2 * f + k + 1) * Q], hsem.at[2 * f + k]
            )
            load.start()
            loads.append(load)
    x_load = pltpu.make_async_copy(x_ref.at[:, pl.ds(2 * t, 2)], xall.at[t], xlocal)
    x_load.start()

    land[...] = jnp.zeros(land.shape, bf16)
    barrier = pltpu.get_barrier_semaphore()
    pl.semaphore_signal(barrier, inc=1, device_id=(s, other), device_id_type=MESH)
    for held, row in ((s > 0, before), (s < ns - 1, after)):
        @pl.when(held)
        def _():
            for k in range(2):
                pl.semaphore_signal(barrier, inc=1, device_id=(row, k), device_id_type=MESH)

    pl.semaphore_wait(
        barrier, 1 + 2 * (s > 0).astype(jnp.int32) + 2 * (s < ns - 1).astype(jnp.int32)
    )
    x_copy = pltpu.make_async_remote_copy(
        src_ref=x_ref.at[:, pl.ds(2 * other, 2)], dst_ref=xall.at[t], send_sem=xsend,
        recv_sem=xrecv, device_id=(s, other), device_id_type=MESH,
    )
    x_copy.start()

    for load in small:
        load.wait()
    scale, shift = 1.0 + mod[1:2, :], mod[0:1, :]
    scaled_sum, shift_sum = jnp.zeros((Q, 128), f32), jnp.zeros((Q, 128), f32)
    for k in range(32):
        at = slice(k * 128, (k + 1) * 128)
        plain = jnp.concatenate(
            [wbuf[n * 16 : n * 16 + 16, at].astype(f32) for n in (0, 2, 1, 3)], axis=0
        )
        scaled = (plain * scale[:, at]).astype(bf16)
        wmat[:, at] = scaled
        scaled_sum = scaled_sum + scaled.astype(f32)
        shift_sum = shift_sum + plain * shift[:, at]
    totals = jnp.sum(
        jnp.transpose(jnp.concatenate([scaled_sum, shift_sum], axis=0)), axis=0, keepdims=True
    )
    bias = jnp.concatenate(
        [bias_in[:, n * 16 : n * 16 + 16] for n in (0, 2, 1, 3)], axis=1
    )
    column_sum, constant = totals[:, :Q], totals[:, Q:] + bias
    guidance, sigma = scalars[0], scalars[1]

    for load in loads:
        load.wait()
    product = lax.dot_general(hbuf[...], wmat[...], NT, preferred_element_type=f32)
    statistics = []
    for f in range(4):
        rows = hbuf[2 * f * Q : 2 * (f + 1) * Q]
        pivot = rows[:, 0:1].astype(f32)
        first, second = jnp.zeros((2 * Q, 128), f32), jnp.zeros((2 * Q, 128), f32)
        for k in range(32):
            part = rows[:, k * 128 : (k + 1) * 128].astype(f32) - pivot
            first = first + part
            second = second + part * part
        offset = jnp.sum(first, axis=1, keepdims=True) * (1.0 / 4096)
        spread = jnp.sum(second, axis=1, keepdims=True) * (1.0 / 4096) - offset * offset
        statistics.append((pivot + offset, lax.rsqrt(jnp.maximum(spread, 0.0) + norm_eps)))
    predictions = []
    for f in range(4):
        centre, inverse = statistics[f]
        branch = inverse * (product[2 * f * Q : 2 * (f + 1) * Q] - centre * column_sum)
        cond, uncond = branch[:Q], branch[Q:]
        predictions.append(uncond + guidance * (cond - uncond) + constant)

    x_load.wait()
    x_copy.wait()
    xt[...] = jnp.transpose(xall[...].reshape(128, 128))
    even, odd = xt[pl.ds(0, Q, stride=2), :], xt[pl.ds(1, Q, stride=2), :]
    for pair in range(2):
        latents = []
        for f in (2 * pair, 2 * pair + 1):
            at = slice(32 * f, 32 * f + 32)
            noisy = jnp.concatenate([even[:, at], odd[:, at]], axis=1)
            latents.append(noisy - sigma * predictions[f])
        lat[pair] = jnp.concatenate(latents, axis=1).astype(bf16)

    def send(peer, to, slot, k):
        count = 1 + to
        return pltpu.make_async_remote_copy(
            src_ref=lat.at[pl.ds(0, count)], dst_ref=land.at[slot, pl.ds(3 - count, count)],
            send_sem=ssem.at[k], recv_sem=rsem.at[slot], device_id=peer, device_id_type=MESH,
        )

    def send_row(row, slot, k):
        return [send((row, 1), 1, slot, k), send((row, 0), 0, slot, k + 1)]

    rows_held = ((s > 0, before, 4 + t, 0), (s < ns - 1, after, t, 2))
    for held, row, slot, k in rows_held:
        @pl.when(held)
        def _():
            for copy in send_row(row, slot, k):
                copy.start()
    for to in range(2):
        @pl.when(other == to)
        def _():
            send((s, to), to, 3 - to, 4).start()

    at = lax.broadcasted_iota(jnp.int32, (256, 256), 0)
    to = lax.broadcasted_iota(jnp.int32, (256, 256), 1)
    turn = (to // 16 + 3) % 4
    source = (turn // 2) * 128 + (to // 128) * 64 + (turn % 2) * 32 + ((to // 64) % 2) * 16 + to % 16
    widen = (at == source).astype(f32).astype(bf16)

    for me in range(2):
        @pl.when(t == me)
        def _():
            count = 1 + me
            land[2 + me, 3 - count : 3] = lat[0:count]
            send((s, other), me, 3 - me, 4).wait_recv()
            send((s, other), 1 - me, 2 + me, 4).wait_send()
            for held, slots in ((s > 0, (0, 1)), (s < ns - 1, (4, 5))):
                @pl.when(held)
                def _():
                    for slot in slots:
                        send((s, other), me, slot, 4).wait_recv()
    for held, row, slot, k in rows_held:
        @pl.when(held)
        def _():
            for copy in send_row(row, slot, k):
                copy.wait_send()

    position = lax.broadcasted_iota(jnp.int32, (Q, 128), 0)
    wide_lane = lax.broadcasted_iota(jnp.int32, (Q, 128), 1)
    parts = []
    for p in range(6):
        for pair in (1, 2):
            here = land[p, pair].astype(f32)
            from_left = jnp.where(position == 0, 0.0, pltpu.roll(here, 1, 0))
            from_right = jnp.where(position == Q - 1, 0.0, pltpu.roll(here, Q - 1, 0))
            beside = jnp.where((wide_lane // 32) % 2 == 0, from_right, from_left)
            parts.append(jnp.concatenate([here, beside], axis=1).astype(bf16))
    wide[...] = jnp.dot(
        jnp.concatenate(parts, axis=0), widen, preferred_element_type=f32
    ).astype(bf16).reshape(6, 2, Q, 256)
    for p in range(4):
        for f in range(2, 6):
            at = slice(f % 2 * 128, f % 2 * 128 + 128)
            above, own, below = [wide[p + k, f // 2 - 1, :, at] for k in range(3)]
            beside = jnp.where(wide_lane < 64, below.astype(f32), above.astype(f32)).astype(bf16)
            windows[p, f - 2] = jnp.concatenate([own, beside], axis=1)


def decoder_kernel(
    windows_ref, win_ref, bin_ref, gain_ref, wmid_ref, bmid_ref, wup_ref, bup_ref, out_ref,
    windows, win, wp, vectors, wm, wu, comps, skip, staged, mixed, pending, fine,
    wrow, wphase, stage, lsem, wsem, vsem, msem, usem, osem,
):
    s, t = lax.axis_index("space"), lax.axis_index("tm")
    ns = lax.axis_size("space")
    others = [
        pltpu.make_async_copy(windows_ref, windows.at[:, 2:6], lsem),
        pltpu.make_async_copy(win_ref, win, wsem),
    ]
    for n, ref in enumerate((bin_ref, gain_ref, bmid_ref, bup_ref)):
        others.append(pltpu.make_async_copy(ref, vectors.at[n], vsem.at[n]))
    for load in others:
        load.start()

    wp[...] = jnp.zeros(wp.shape, bf16)
    windows[:, 0:2] = jnp.zeros((4, 2, Q, 256), bf16)
    for load in others:
        load.wait()
    mids = [pltpu.make_async_copy(wmid_ref.at[i], wm.at[i], msem.at[i]) for i in range(3)]
    up_load = pltpu.make_async_copy(wup_ref, wu, usem)
    for load in mids + [up_load]:
        load.start()
    for i in range(3):
        for j in range(3):
            block = win[i, j]
            for a in range(2):
                for b in range(2):
                    at = i * 256 + ((a + j - 1) % 4) * 64 + b * 16
                    wp[at : at + 48, (2 * a + b) * CH : (2 * a + b + 1) * CH] = block

    bias_first, half_gain = vectors[0], 0.5 * vectors[1]
    bias_mid, bias_up = vectors[2], vectors[3]
    frame = lax.broadcasted_iota(jnp.int32, (4 * Q, 1), 0) // Q
    frame_held = jnp.logical_or(frame >= 2, t > 0)

    def patch_row(p, _):
        lhs = jnp.concatenate(
            [windows[p, i : i + 4].reshape(4 * Q, 256) for i in range(3)], axis=1
        )
        for a in range(2):
            line = 2 * p + a
            held = jnp.logical_and(4 * s - 2 + line >= 0, 4 * s - 2 + line < 4 * ns)
            mask = jnp.where(jnp.logical_and(frame_held, held), 1.0, 0.0)
            sides = []
            for b in range(2):
                column = (2 * a + b) * CH
                value = jnp.dot(
                    lhs, wp[:, column : column + CH], preferred_element_type=f32
                ) + bias_first
                for f in range(2):
                    skip[f, b, line] = value[(2 + f) * Q : (3 + f) * Q].astype(bf16)
                power = jnp.mean(value * value, axis=1, keepdims=True)
                half = value * (lax.rsqrt(power + norm_eps) * mask) * half_gain
                active = half * jnp.tanh(half) + half
                a0, a1, a2, a3 = [active[f * Q : (f + 1) * Q] for f in range(4)]
                sides.append((a0 - a2, a1 + a2, a2 - a1, a1 - a3))
            for k in range(4):
                even, odd = sides[0][k], sides[1][k]
                comps[4 * k, line] = (moved_down(odd) - odd).astype(bf16)
                comps[4 * k + 1, line] = (even + odd).astype(bf16)
                comps[4 * k + 2, line] = (odd - even).astype(bf16)
                comps[4 * k + 3, line] = (even - moved_up(even)).astype(bf16)
        return 0

    for p in range(4):
        patch_row(p, 0)

    def finish(f, b, n, middle):
        cols = slice(n * 256, (n + 1) * 256)
        for r in range(6):
            line = 4 * s - 1 + r
            held = jnp.where(jnp.logical_and(line >= 0, line < 4 * ns), 1.0, 0.0)
            value = (
                skip[f, b, r + 1, :, cols].astype(f32)
                + middle[r * Q : (r + 1) * Q]
                + bias_mid[:, cols]
            ) * held
            rounded = value.astype(bf16)
            fine[f, r, b, :, cols] = rounded
            if b == 1:
                odd, even = rounded.astype(f32), fine[f, r, 0, :, cols].astype(f32)
                fine[f, r, 2, :, cols] = (even - moved_down(odd)).astype(bf16)
                fine[f, r, 3, :, cols] = (odd - even).astype(bf16)
                fine[f, r, 4, :, cols] = (moved_up(even) - odd).astype(bf16)

    def phase_weights(a):
        both = (wu.at[1], wu.at[2]) if a == 0 else (wu.at[0], wu.at[1])
        alone = wu.at[2 * a]
        wrow[...] = both[0][...] + both[1][...]
        for i in range(2):
            held = alone if i == a else wrow
            k0, k1, k2 = [held[k * CH : (k + 1) * CH] for k in range(3)]
            for n, value in enumerate((k0, k0 + k1 + k2, k2)):
                wphase[a, n, i] = value

    for k in range(4):
        if k == 0:
            mids[0].wait()
        if k == 1:
            mids[1].wait()
            mids[2].wait()
            up_load.wait()
        if k > 1:
            phase_weights(k - 2)
        source = wm.at[0] if k == 0 else wm.at[2] if k == 3 else staged
        if k in (1, 2):
            for j in range(3):
                ends = wm[0, j] + wm[2, j]
                staged[j] = ends + wm[1, j] if k == 1 else ends - wm[1, j]
        for j in range(3):
            left, centre, right = [source[j, c * CH : (c + 1) * CH] for c in range(3)]
            mixed[k % 2, 0, j * CH : (j + 1) * CH] = left + right + centre
            mixed[k % 2, 1, j * CH : (j + 1) * CH] = left + right - centre
        for n in range(2):
            cols = slice(n * 256, (n + 1) * 256)
            products = []
            for c in range(4):
                lhs = jnp.concatenate(
                    [comps[4 * k + c, j : j + 6].reshape(6 * Q, CH) for j in range(3)], axis=1
                )
                if c in (1, 2):
                    rhs = mixed[k % 2, c - 1, :, cols]
                else:
                    at = 0 if c == 0 else 2 * CH
                    rhs = jnp.concatenate(
                        [source[j, at : at + CH, cols] for j in range(3)], axis=0
                    )
                products.append(jnp.dot(lhs, rhs, preferred_element_type=f32))
            m0, m1, m2, m3 = products
            for b, total in enumerate((m0 + 0.5 * (m1 + m2), 0.5 * (m1 - m2) - m3)):
                if k == 0:
                    pending[0, b, :, cols] = total
                elif k == 1:
                    pending[1, b, :, cols] = total
                elif k == 2:
                    held = pending[1, b, :, cols]
                    pending[1, b, :, cols] = 0.5 * (held - total)
                    finish(0, b, n, pending[0, b, :, cols] + 0.5 * (held + total))
                else:
                    finish(1, b, n, pending[1, b, :, cols] - total)

    writes = []

    def write_lines(f, a):
        for r in range(4):
            line = 8 * a + 4 * f + r
            for g in range(4):
                comps[line, 0:4, :, g * 128 : (g + 1) * 128] = stage[a, r, g].astype(bf16).reshape(
                    4, Q, 128
                )
            write = pltpu.make_async_copy(
                comps.at[line, 0:4], out_ref.at[f, r, a], osem.at[line]
            )
            write.start()
            writes.append(write)

    behind = None
    for f in range(2):
        for a in range(2):
            for n in range(2):
                cols = slice(n * 256, (n + 1) * 256)
                products = []
                for kind, at in enumerate((2, 0, 3)):
                    lhs = jnp.concatenate(
                        [
                            fine[f, a + i : a + i + 4, at : at + 2].reshape(8 * Q, CH)
                            for i in range(2)
                        ],
                        axis=1,
                    )
                    rhs = wphase[a, kind, :, :, cols].reshape(2 * CH, 256)
                    products.append(jnp.dot(lhs, rhs, preferred_element_type=f32))
                first, centre, last = products
                centre = centre + bias_up[:, cols]
                for b, value in enumerate((centre - first, centre + last)):
                    for r in range(4):
                        for side in range(2):
                            at = (2 * r + side) * Q
                            for g in range(2):
                                stage[a, r, 2 * n + g, pl.ds(2 * side + b, Q, stride=4), :] = value[
                                    at : at + Q, g * 128 : (g + 1) * 128
                                ]
            if behind is not None:
                write_lines(*behind)
            behind = (f, a)
    write_lines(*behind)
    for write in writes:
        write.wait()


def on_device(
    hidden, modulation, w_proj, b_proj, guidance, x_noisy, sigma, w_in, b_in, gain,
    w_mid, b_mid, w_up, b_up,
):
    vmem = pl.BlockSpec(memory_space=pltpu.VMEM)
    anywhere = pl.BlockSpec(memory_space=pltpu.HBM)
    rows = lambda v: v.reshape(1, -1)
    dma = pltpu.SemaphoreType.DMA
    windows = pl.pallas_call(
        latent_kernel,
        out_shape=jax.ShapeDtypeStruct((4, 4, Q, 256), bf16),
        in_specs=[anywhere] * 7,
        out_specs=vmem,
        scratch_shapes=[
            pltpu.VMEM((8 * Q, 4096), bf16),
            pltpu.VMEM((64, 4096), bf16),
            pltpu.VMEM((2, 4096), f32),
            pltpu.VMEM((64, 4096), bf16),
            pltpu.VMEM((1, 64), f32),
            pltpu.VMEM((2, 1, 1), f32),
            pltpu.VMEM((2, 2, 2, 16, 128), f32),
            pltpu.VMEM((128, 128), f32),
            pltpu.VMEM((2, Q, 128), bf16),
            pltpu.VMEM((6, 3, Q, 128), bf16),
            pltpu.VMEM((6, 2, Q, 256), bf16),
            dma((8,)), dma((5,)), dma, dma, dma, dma((5,)), dma((6,)),
        ],
        compiler_params=pltpu.CompilerParams(
            collective_id=0, has_side_effects=True, vmem_limit_bytes=60 << 20
        ),
    )(
        hidden, modulation, w_proj.T, rows(b_proj), rows(guidance), rows(sigma),
        jnp.swapaxes(x_noisy, 2, 3),
    )
    decoded = pl.pallas_call(
        decoder_kernel,
        out_shape=jax.ShapeDtypeStruct((2, 4, 2, 4, Q, CH), bf16),
        in_specs=[anywhere] * 8,
        out_specs=anywhere,
        scratch_shapes=[
            pltpu.VMEM((4, 6, Q, 256), bf16),
            pltpu.VMEM((3, 3, 48, CH), bf16),
            pltpu.VMEM((768, 4 * CH), bf16),
            pltpu.VMEM((4, 1, CH), f32),
            pltpu.VMEM((3, 3, 3 * CH, CH), bf16),
            pltpu.VMEM((3, 3 * CH, CH), bf16),
            pltpu.VMEM((16, 8, Q, CH), bf16),
            pltpu.VMEM((2, 2, 8, Q, CH), bf16),
            pltpu.VMEM((3, 3 * CH, CH), bf16),
            pltpu.VMEM((2, 2, 3 * CH, CH), bf16),
            pltpu.VMEM((2, 2, 6 * Q, CH), f32),
            pltpu.VMEM((2, 6, 5, Q, CH), bf16),
            pltpu.VMEM((3 * CH, CH), bf16),
            pltpu.VMEM((2, 3, 2, CH, CH), bf16),
            pltpu.VMEM((2, 4, 4, 256, 128), f32),
            dma, dma, dma((4,)), dma((3,)), dma, dma((16,)),
        ],
        compiler_params=pltpu.CompilerParams(vmem_limit_bytes=62 << 20),
    )(windows, w_in, rows(b_in), rows(gain), w_mid, rows(b_mid), w_up, rows(b_up))
    return decoded.reshape(2, 8, 256, CH)


def solution(mesh):
    return jax.shard_map(
        on_device,
        mesh=mesh,
        in_specs=(
            P(None, None, ("space", "tm"), None), P(), P(), P(), P(),
            P("tm", "space", None, None), P(), P(), P(), P(), P(), P(), P(), P(),
        ),
        out_specs=P("tm", "space", None, None),
        check_vma=False,
    )
```
